128 devices in a mesh: group: 4 (over y), tp: 32 (over z, x, core).
Axes of the slice: x: 4, y: 4, z: 4, core: 2. Of those that a mesh axis runs over, the one named last changes fastest.
Arguments:
- tokens: bfloat16 [8192, 8192], P(('group', 'tp')), may hold values from -6 to 6
- query_weight_matrix: bfloat16 [8192, 8192], P(None, 'tp'), may hold values from -0.0625 to 0.0625
- adapter_down_weight: bfloat16 [512, 64, 8192], P('group', 'tp'), may hold values from -0.0625 to 0.0625
- adapter_up_weight: bfloat16 [512, 64, 8192], P('group', None, 'tp'), may hold values from -0.75 to 0.75
- lengths: int32 [4, 16], replicated, may hold values from 1 to 1024, 2048 in all within a row
- request_adapter_id: int32 [4, 16], replicated, may hold values from 0 to 511, as said below
- adapter_storage_slot: int32 [512], replicated, may hold values from 0 to 511, as said below
Outputs:
- query: bfloat16 [8192, 8192], P('group', 'tp')
The draws below stay inside these ranges and needn't reach their ends.
Inputs may be any that keep to these rules, and one draw needn't show every extreme that they name: `request_adapter_id`: no more than 6 requests of one group use adapters whose slots lie on one owner group (slot s lies on owner group s // 128); every group reaches 6 on some owner group. `adapter_storage_slot`: A permutation of the slots.
All inputs are finite; a program needn't handle non-finite values.
Results may differ from the reference program's by a relative error of at most 0.003.
Values may be sent and summed in bfloat16 or wider, within the bound.
A program may use at most 192 MiB of HBM per device.

```python
import math
import jax
import jax.numpy as jnp
import numpy as np
from jax import lax

MODEL_WIDTH = 8192
QUERY_FEATURES = 8192
ADAPTER_RANK = 64
GROUP_REQUESTS = 16
CAP = 6
ADP_G = 128
GROUPS = 4
T_GROUP = 2048
TOKENS = 8192
ADAPTER_TOTAL = 512
MAXLEN = 1024


def shared_slots(key):
    return jax.random.permutation(key, ADAPTER_TOTAL).astype(jnp.int32)


def draw_adapter_storage_slot(key, part):
    request_slots = shared_slots(key)
    return request_slots


def draw_request_adapter_id(key, part):
    request_slots = shared_slots(key)
    key = jax.random.fold_in(key, 11)
    first_key, second_key, third_key = jax.random.split(key, 3)
    busiest = jax.random.randint(first_key, (GROUPS,), 0, GROUPS).astype(jnp.int32)
    spare = jnp.repeat(jnp.arange(GROUPS - 1, dtype=jnp.int32), CAP)

    def one_group(group_key, top):
        spare_key, order_key = jax.random.split(group_key)
        others = (top + 1 + jax.random.permutation(spare_key, spare)) % GROUPS
        owners = jnp.concatenate([jnp.full((CAP,), top, jnp.int32), others[:GROUP_REQUESTS - CAP]])
        return owners[jax.random.permutation(order_key, GROUP_REQUESTS)].astype(jnp.int32)
    owners = jax.vmap(one_group)(jax.random.split(second_key, GROUPS), busiest)
    order = jnp.arange(GROUP_REQUESTS, dtype=jnp.int32)
    same_owner = owners[:, :, None] == owners[:, None, :]
    earlier = order[None, :] < order[:, None]
    rank_in = jnp.sum((same_owner & earlier[None]).astype(jnp.int32), axis=2)
    tables = jax.vmap(lambda table_key: jax.random.permutation(table_key, ADP_G))(jax.random.split(third_key, GROUPS * GROUPS))
    tables = tables.reshape(GROUPS, GROUPS, ADP_G).astype(jnp.int32)
    group_index = jnp.arange(GROUPS, dtype=jnp.int32)[:, None]
    local = tables[group_index, owners, rank_in]
    slot_of = owners * ADP_G + local
    inverse = jnp.argsort(request_slots).astype(jnp.int32)
    return inverse[slot_of].astype(jnp.int32)


def level_of(rng, extent, pieces, smallest, largest):
    gain = 1.0
    for dim, blocks in pieces:
        heights = jax.random.uniform(jax.random.fold_in(jax.random.fold_in(rng, 6), dim), (blocks,), jnp.float32, smallest / len(pieces), largest / len(pieces))
        gain = gain * jnp.repeat(jnp.exp(heights), extent[dim] // blocks).reshape((-1,) + (1,) * (len(extent) - 1 - dim))
    return gain


def length_profile(amount, total, reach, slope):
    portions = [(1 << 20) // math.isqrt(standing ** slope) + 1 for standing in range(2, amount + 1)]
    spare, given = total - reach - (amount - 1), [1] * (amount - 1)
    while spare > 0:
        candidates = [i for i in range(amount - 1) if given[i] < reach]
        pool, left = sum([portions[i] for i in candidates]), spare
        for i in candidates:
            more = min(reach - given[i], max(1, left * portions[i] // pool), spare)
            given[i] = given[i] + more
            spare = spare - more
    return np.array([reach] + given)


def ragged(key, count, total, bound, slope):
    if count == 2:
        one = jax.random.randint(key, (), max(1, total - bound), min(bound, total - 1) + 1)
        return jnp.stack([one, total - one])
    sizes = jnp.asarray(length_profile(count, total, bound, slope), jnp.int32)
    twos = (count - 1) // 2
    giver, sink = sizes[1:1 + 2 * twos:2], sizes[2:2 + 2 * twos:2]
    slack = jnp.minimum(giver - 1, bound - sink)
    passed = jax.random.randint(jax.random.fold_in(key, 1), (twos,), 0, 1 << 20) % (slack + 1)
    sizes = sizes.at[1:1 + 2 * twos:2].set(giver - passed).at[2:2 + 2 * twos:2].set(sink + passed)
    return sizes[jax.random.permutation(jax.random.fold_in(key, 2), count)]


def centred(rng, shape, scale, most, shards=(), kind=jnp.bfloat16):
    drawn = scale * jax.random.normal(rng, shape, jnp.float32)
    if shards:
        drawn = drawn * level_of(rng, shape, shards, -0.22, 0.18)
    return jnp.clip(drawn, -most, most).astype(kind)


def setup_inputs(seed: int = 0) -> dict:
    key_list = jax.random.split(jax.random.key(seed), 8)
    tokens = centred(key_list[0], (TOKENS, MODEL_WIDTH), 1.0, 6.0, ((0, 128),))
    query_weight_matrix = centred(key_list[1], (MODEL_WIDTH, QUERY_FEATURES), MODEL_WIDTH ** -0.5, 0.0625, ((1, 32),))
    adapter_down_weight = centred(key_list[2], (ADAPTER_TOTAL, ADAPTER_RANK, MODEL_WIDTH), MODEL_WIDTH ** -0.5, 0.0625, ((0, 4), (1, 32)))
    adapter_up_weight = centred(key_list[3], (ADAPTER_TOTAL, ADAPTER_RANK, QUERY_FEATURES), ADAPTER_RANK ** -0.5, 0.75, ((0, 4), (2, 32)))
    lengths = jax.vmap(lambda own: ragged(own, GROUP_REQUESTS, T_GROUP, MAXLEN, 2))(jax.random.split(key_list[4], GROUPS)).reshape((GROUPS, GROUP_REQUESTS)).astype(jnp.int32)
    request_adapter_id = draw_request_adapter_id(jax.random.fold_in(key_list[7], 71), 0)
    adapter_storage_slot = draw_adapter_storage_slot(jax.random.fold_in(key_list[7], 71), 0)
    return {"tokens": tokens, "query_weight_matrix": query_weight_matrix, "adapter_down_weight": adapter_down_weight, "adapter_up_weight": adapter_up_weight, "lengths": lengths, "request_adapter_id": request_adapter_id, "adapter_storage_slot": adapter_storage_slot}


def reference(tokens, query_weight_matrix, adapter_down_weight, adapter_up_weight, lengths, request_adapter_id, adapter_storage_slot):
    position = jnp.arange(T_GROUP, dtype=jnp.int32)
    ends = jnp.cumsum(lengths, axis=1).astype(jnp.int32)
    request_of = jnp.sum((position[None, :, None] >= ends[:, None, :]).astype(jnp.int32), axis=2).astype(jnp.int32)
    slot_req = adapter_storage_slot[request_adapter_id]
    order = jnp.arange(GROUP_REQUESTS, dtype=jnp.int32)
    rows_by_group = tokens.reshape(GROUPS, T_GROUP, MODEL_WIDTH)

    def one_group(inputs):
        rows, request_slots, belongs = inputs
        down_per_request = adapter_down_weight[request_slots].reshape(GROUP_REQUESTS * ADAPTER_RANK, MODEL_WIDTH)
        up_per_request = adapter_up_weight[request_slots].reshape(GROUP_REQUESTS * ADAPTER_RANK, QUERY_FEATURES)
        base_output = jnp.dot(rows, query_weight_matrix, preferred_element_type=jnp.float32)
        partial_value = jnp.dot(rows, down_per_request.T, preferred_element_type=jnp.float32)
        onehot = (belongs[:, None] == order[None, :]).astype(jnp.float32)
        shrink = jnp.sum(partial_value.reshape(T_GROUP, GROUP_REQUESTS, ADAPTER_RANK) * onehot[:, :, None], axis=1).astype(jnp.bfloat16)
        spread = (onehot.astype(jnp.bfloat16)[:, :, None] * shrink[:, None, :]).reshape(T_GROUP, GROUP_REQUESTS * ADAPTER_RANK)
        adapter_update = jnp.dot(spread, up_per_request, preferred_element_type=jnp.float32)
        return (base_output + 0.5 * adapter_update).astype(jnp.bfloat16)

    query = lax.map(one_group, (rows_by_group, slot_req, request_of))
    return query.reshape(TOKENS, QUERY_FEATURES)
```

```python
import jax
import jax.numpy as jnp
from jax import lax
from jax.experimental import pallas as pl
from jax.experimental.pallas import tpu as pltpu
from jax.sharding import PartitionSpec as P

MESH = pl.DeviceIdType.MESH
F32 = jnp.float32
BF16 = jnp.bfloat16

CAP = 6
GROUPS = 4
REQUESTS = 16
RANK = 64
WIDTH = 8192
COLS = 256
SHARD = 64
HALVES = 2
HALF = SHARD // HALVES
SOURCES = 8
HROWS = SOURCES * HALF
NK = 4
KC = WIDTH // NK
WC = KC // 4
PIECES = HALVES * NK
OWNED = 128

LEFT, RIGHT, FAR, ACROSS, ACROSS_LEFT, ACROSS_RIGHT, ACROSS_FAR = range(7)


def kernel(
    tok_hbm, w_hbm, down_hbm, up_hbm, len_ref, rid_ref, slot_ref, out_hbm,
    tok, wbuf, dloc, uloc, dsend, usend, drecv, urecv, dtmp, dc, uc, acc, part, shr, ost,
    loc_sem, own_sem, tok_ss, tok_rs, w_ss, w_rs, ws_ss, ws_rs, wf_ss, wf_rs,
    ad_ss, ad_rs, cp_ss, cp_rs, sh_ss, sh_rs, out_ss, out_rs,
):
    g = lax.axis_index("group")
    tp = lax.axis_index("tp")
    z = tp // 8
    x = (tp // 2) % 4
    c = tp % 2
    side = z // 2
    bit = z % 2
    z_across = 2 * side + 1 - bit
    z_partner = 3 - z

    def device(zz, xx, cc, gg=None):
        return (g if gg is None else gg, (zz * 4 + xx) * 2 + cc)

    left, right, far = (x + 3) % 4, (x + 1) % 4, (x + 2) % 4
    to_left, to_right = device(z, left, c), device(z, right, c)
    to_across = device(z_across, x, c)
    to_sibling = device(z, x, 1 - c)
    to_partner = device(z_partner, x, c)
    to_partner_other = device(z_partner, x, 1 - c)

    sends = []

    def send(src, dst, ss, rs, dev):
        copy = pltpu.make_async_remote_copy(
            src_ref=src, dst_ref=dst, send_sem=ss, recv_sem=rs, device_id=dev, device_id_type=MESH
        )
        copy.start()
        sends.append(copy)

    def arrived(dst, rs):
        pltpu.make_async_copy(dst, dst, rs).wait()

    down_copy = pltpu.make_async_copy(down_hbm, dloc, loc_sem.at[0])
    up_copy = pltpu.make_async_copy(up_hbm, uloc, loc_sem.at[1])
    mine = bit * 4 + x
    tok_copy = pltpu.make_async_copy(tok_hbm, tok.at[mine], loc_sem.at[2])
    w_copies = [
        pltpu.make_async_copy(
            w_hbm.at[pl.ds(i * KC, KC)], wbuf.at[0, pl.ds(i * KC, KC)], own_sem.at[i]
        )
        for i in range(NK)
    ]
    down_copy.start()
    up_copy.start()
    tok_copy.start()
    for copy in w_copies:
        copy.start()

    peers = [device(z, xx, c) for xx in (left, right, far)]
    peers += [device(z_across, xx, c) for xx in (x, left, right, far)]
    near = list(peers)
    peers += [to_sibling, to_partner, to_partner_other]
    peers += [device(z, x, c, (g + d) % GROUPS) for d in (1, 2, 3)]
    barrier = pltpu.get_barrier_semaphore()
    for dev in peers:
        pl.semaphore_signal(barrier, inc=1, device_id=dev, device_id_type=MESH)
    pl.semaphore_wait(barrier, len(peers))

    def at(source, p):
        r, k = divmod(p, NK)
        return tok.at[source, pl.ds(r * HALF, HALF), pl.ds(k * KC, KC)]

    def tok_send(source, p, n, cls, dev):
        send(at(source, p), at(source, p), tok_ss.at[n, p], tok_rs.at[cls, p], dev)

    s_left, s_right, s_far = bit * 4 + left, bit * 4 + right, bit * 4 + far
    other = (1 - bit) * 4
    a_mine, a_left, a_right, a_far = other + x, other + left, other + right, other + far

    def across_first(p):
        return p % 2 == 0

    def relay_right(p):
        return (p // 2) % 2 == 0

    def own_send(p):
        r, k = divmod(p, NK)
        src = tok_hbm.at[pl.ds(r * HALF, HALF), pl.ds(k * KC, KC)]
        send(src, at(mine, p), tok_ss.at[0, p], tok_rs.at[ACROSS, p], to_across)
        send(src, at(mine, p), tok_ss.at[1, p], tok_rs.at[LEFT, p], to_right)
        send(src, at(mine, p), tok_ss.at[2, p], tok_rs.at[RIGHT, p], to_left)

    def tok_first(p):
        arrived(at(a_mine, p), tok_rs.at[ACROSS, p])
        if across_first(p):
            tok_send(a_mine, p, 3, ACROSS_LEFT, to_right)
            tok_send(a_mine, p, 4, ACROSS_RIGHT, to_left)
        arrived(at(s_left, p), tok_rs.at[LEFT, p])
        if relay_right(p):
            tok_send(s_left, p, 5, FAR, to_right)
        if not across_first(p):
            tok_send(s_left, p, 3, ACROSS_LEFT, to_across)
        arrived(at(s_right, p), tok_rs.at[RIGHT, p])
        if not relay_right(p):
            tok_send(s_right, p, 5, FAR, to_left)
        if not across_first(p):
            tok_send(s_right, p, 4, ACROSS_RIGHT, to_across)

    def tok_second(p):
        if across_first(p):
            arrived(at(a_left, p), tok_rs.at[ACROSS_LEFT, p])
            if relay_right(p):
                tok_send(a_left, p, 6, ACROSS_FAR, to_right)
            arrived(at(a_right, p), tok_rs.at[ACROSS_RIGHT, p])
            if not relay_right(p):
                tok_send(a_right, p, 6, ACROSS_FAR, to_left)
            arrived(at(s_far, p), tok_rs.at[FAR, p])
        else:
            arrived(at(s_far, p), tok_rs.at[FAR, p])
            tok_send(s_far, p, 6, ACROSS_FAR, to_across)
            arrived(at(a_left, p), tok_rs.at[ACROSS_LEFT, p])
            arrived(at(a_right, p), tok_rs.at[ACROSS_RIGHT, p])

    def tok_third(p):
        arrived(at(a_far, p), tok_rs.at[ACROSS_FAR, p])

    def w_rows(i, q):
        return pl.ds(i * KC + q * WC, WC)

    def w_own_send(i):
        rows = w_rows(i, g)
        send(w_hbm.at[rows], wbuf.at[2, rows], w_ss.at[0, i], w_rs.at[0, i], to_partner)

    def w_sibling_send(i):
        rows = pl.ds(i * KC, KC)
        send(w_hbm.at[rows], wbuf.at[1, rows], ws_ss.at[i], ws_rs.at[i], to_sibling)

    g_next, g_prev, g_far = (g + 1) % GROUPS, (g + 3) % GROUPS, (g + 2) % GROUPS
    to_next, to_prev = device(z, x, c, g_next), device(z, x, c, g_prev)

    def w_forward(i, q, cls):
        rows = w_rows(i, q)
        send(wbuf.at[2, rows], wbuf.at[3, rows], wf_ss.at[cls, i], wf_rs.at[cls, i], to_sibling)

    def w_send(i, q, n, cls, dev):
        rows = w_rows(i, q)
        send(wbuf.at[2, rows], wbuf.at[2, rows], w_ss.at[n, i], w_rs.at[cls, i], dev)

    def w_first(i):
        arrived(wbuf.at[2, w_rows(i, g)], w_rs.at[0, i])
        w_send(i, g, 1, 1, to_next)
        w_send(i, g, 2, 3, to_prev)
        w_forward(i, g, 0)

    def w_second(i):
        arrived(wbuf.at[2, w_rows(i, g_prev)], w_rs.at[1, i])
        if i % 2 == 0:
            w_send(i, g_prev, 3, 2, to_next)
        w_forward(i, g_prev, 1)
        arrived(wbuf.at[2, w_rows(i, g_next)], w_rs.at[3, i])
        if i % 2 == 1:
            w_send(i, g_next, 3, 2, to_prev)
        w_forward(i, g_next, 3)

    def w_third(i):
        arrived(wbuf.at[2, w_rows(i, g_far)], w_rs.at[2, i])
        w_forward(i, g_far, 2)

    def w_ready(i):
        w_copies[i].wait()
        arrived(wbuf.at[1, pl.ds(i * KC, KC)], ws_rs.at[i])
        for cls, q in enumerate((g, g_prev, g_far, g_next)):
            arrived(wbuf.at[3, w_rows(i, q)], wf_rs.at[cls, i])

    def adapters_pick():
        picked = []
        for dest in range(GROUPS):
            index = [jnp.int32(0)] * CAP
            count = jnp.int32(0)
            for j in range(REQUESTS):
                slot = slot_ref[rid_ref[dest, j]]
                is_mine = slot // OWNED == g
                local = slot % OWNED
                for p in range(min(CAP, j + 1)):
                    index[p] = jnp.where(is_mine & (count == p), local, index[p])
                count = count + is_mine.astype(jnp.int32)
            picked.append(index)
        down_copy.wait()
        for dest in range(GROUPS):
            for p in range(CAP):
                dsend[dest * CAP + p] = dloc[picked[dest][p]]
        for d in (1, 3, 2):
            rows = pl.ds(((g + d) % GROUPS) * CAP, CAP)
            dev = device(z, x, c, (g + d) % GROUPS)
            send(dsend.at[rows], drecv.at[pl.ds(g * CAP, CAP)], ad_ss.at[0, d], ad_rs.at[0, d], dev)
        up_copy.wait()
        for dest in range(GROUPS):
            for p in range(CAP):
                usend[dest * CAP + p] = uloc[picked[dest][p]]
        for d in (1, 3, 2):
            rows = pl.ds(((g + d) % GROUPS) * CAP, CAP)
            dev = device(z, x, c, (g + d) % GROUPS)
            send(usend.at[rows], urecv.at[pl.ds(g * CAP, CAP)], ad_ss.at[1, d], ad_rs.at[1, d], dev)
        rows = pl.ds(g * CAP, CAP)
        for n, (src, dst) in enumerate(((dsend, drecv), (usend, urecv))):
            pltpu.make_async_copy(src.at[rows], dst.at[rows], ad_ss.at[n, 0]).start()

    def request_places():
        places = []
        counts = [jnp.int32(0)] * GROUPS
        for j in range(REQUESTS):
            owner = slot_ref[rid_ref[g, j]] // OWNED
            place = jnp.int32(0)
            for o in range(GROUPS):
                hit = owner == o
                place = place + jnp.where(hit, o * CAP + counts[o], 0)
                counts[o] = counts[o] + hit.astype(jnp.int32)
            places.append(place)
        return places

    def adapters_arrived(n, ref, src):
        rows = pl.ds(g * CAP, CAP)
        pltpu.make_async_copy(src.at[rows], ref.at[rows], ad_ss.at[n, 0]).wait()
        for d in (1, 2, 3):
            arrived(ref.at[pl.ds(((g + 4 - d) % GROUPS) * CAP, CAP)], ad_rs.at[n, d])

    def adapters_share(n, ref):
        send(ref.at[0], ref.at[2], cp_ss.at[n, 0], cp_rs.at[n, 2], to_partner)
        send(ref.at[0], ref.at[1], cp_ss.at[n, 1], cp_rs.at[n, 1], to_sibling)

    def down_compact(places):
        adapters_arrived(0, drecv, dsend)
        for j in range(REQUESTS):
            dtmp[2 * j : 2 * j + 2, :] = drecv[places[j]].astype(F32)
        dc[0] = dtmp[...].astype(BF16)
        adapters_share(0, dc)

    def up_compact(places):
        adapters_arrived(1, urecv, usend)
        for j in range(REQUESTS):
            uc[0, j] = urecv[places[j]]
        adapters_share(1, uc)

    def adapters_forward(n, ref):
        arrived(ref.at[2], cp_rs.at[n, 2])
        send(ref.at[2], ref.at[3], cp_ss.at[n, 2], cp_rs.at[n, 3], to_sibling)

    def adapters_ready(n, ref):
        arrived(ref.at[1], cp_rs.at[n, 1])
        arrived(ref.at[3], cp_rs.at[n, 3])

    def token_block(r, k):
        return tok[:, r * HALF : (r + 1) * HALF, k * KC : (k + 1) * KC].reshape(HROWS, KC)

    def base(r, k):
        block = token_block(r, k)
        for m in range(4):
            term = jnp.dot(block, wbuf[m, k * KC : (k + 1) * KC, :], preferred_element_type=F32)
            if k == 0:
                acc[r, m] = term
            else:
                acc[r, m] += term

    def low_rank(r, k):
        rows = dc[:, :, k * KC : (k + 1) * KC].reshape(4 * 2 * REQUESTS, KC)
        term = lax.dot_general(
            rows, token_block(r, k), (((1,), (1,)), ((), ())), preferred_element_type=F32
        )
        if k == 0:
            part[r] = term
        else:
            part[r] += term

    ends = []
    total = jnp.int32(0)
    for j in range(REQUESTS):
        total = total + len_ref[g, j]
        ends.append(total)

    def request_of(row, r):
        position = side * 1024 + (row // HALF) * 128 + c * SHARD + r * HALF + row % HALF
        request = jnp.zeros(row.shape, jnp.int32)
        for j in range(REQUESTS):
            request = request + jnp.where(position >= ends[j], 1, 0)
        return request

    z_low = jnp.minimum(z, z_partner)
    quad = z_low * 4 + x

    def codes_send(r):
        row = lax.broadcasted_iota(jnp.int32, (128, HROWS), 0)
        request = request_of(lax.broadcasted_iota(jnp.int32, (128, HROWS), 1), r)
        masked = jnp.where(request == (row % 32) // 2, part[r], 0.0).astype(BF16)
        lane = lax.broadcasted_iota(jnp.int32, (16, 128), 1)
        member = lane // 32
        high = jnp.where(z == z_low, member // 2, 1 - member // 2)
        core = jnp.where(c == 0, member % 2, 1 - member % 2)
        place = high * 4 + core * 2 + lane % 2
        pick = jnp.where(place == lax.broadcasted_iota(jnp.int32, (16, 128), 0), 1.0, 0.0)
        codes = jnp.dot(pick.astype(BF16), masked, preferred_element_type=F32)
        shr[r, quad] = codes[:8]
        for n, dev in enumerate(near):
            cls = (RIGHT, LEFT, FAR, ACROSS, ACROSS_RIGHT, ACROSS_LEFT, ACROSS_FAR)[n]
            send(shr.at[r, quad], shr.at[r, quad], sh_ss.at[r, n], sh_rs.at[r, cls], dev)

    def out_piece(zz, cc, r):
        return out_hbm.at[zz // 2, :, cc, pl.ds(r * HALF, HALF), :]

    def out_local(r):
        return pltpu.make_async_copy(ost.at[r, 0], out_piece(z, c, r), loc_sem.at[3 + r])

    def finish(r):
        z_other_low = 1 - z_low
        quad_low, quad_other = z_low * 4, z_other_low * 4
        for cls, q in (
            (LEFT, quad_low + left), (RIGHT, quad_low + right), (FAR, quad_low + far),
            (ACROSS, quad_other + x), (ACROSS_LEFT, quad_other + left),
            (ACROSS_RIGHT, quad_other + right), (ACROSS_FAR, quad_other + far),
        ):
            arrived(shr.at[r, q], sh_rs.at[r, cls])
        place = lax.broadcasted_iota(jnp.int32, (RANK, 128), 0)
        lane = lax.broadcasted_iota(jnp.int32, (RANK, 128), 1) % RANK
        low, xx, rest = place // 32, (place // 8) % 4, place % 8
        zz = jnp.where(rest // 4 == 0, low, 3 - low)
        rank = zz * 16 + xx * 4 + rest % 4
        order = jnp.where(rank == lane, 1.0, 0.0).astype(BF16)
        codes = shr[r].reshape(RANK, HROWS).astype(BF16)
        codes = lax.dot_general(codes, order, (((0,), (0,)), ((), ())), preferred_element_type=F32)
        request = request_of(lax.broadcasted_iota(jnp.int32, (HROWS, 128), 0), r)
        half = lax.broadcasted_iota(jnp.int32, (HROWS, 128), 1) // RANK
        request = request - half
        spread = jnp.concatenate(
            [jnp.where(request == 2 * b, codes, 0.0).astype(BF16) for b in range(REQUESTS // 2)],
            axis=1,
        )
        for m in (2, 3, 1, 0):
            table = uc[m].reshape(REQUESTS * RANK, COLS)
            update = jnp.dot(spread, table, preferred_element_type=F32)
            result = (acc[r, m] + 0.5 * update).astype(BF16)
            ost[r, m] = result.reshape(SOURCES, HALF, COLS)
            if m == 0:
                out_local(r).start()
            else:
                dev = (None, to_sibling, to_partner, to_partner_other)[m]
                send(ost.at[r, m], out_piece(z, c, r), out_ss.at[r, m], out_rs.at[r, m], dev)

    def out_arrived(r):
        out_local(r).wait()
        arrived(out_piece(z, 1 - c, r), out_rs.at[r, 1])
        arrived(out_piece(z_partner, c, r), out_rs.at[r, 2])
        arrived(out_piece(z_partner, 1 - c, r), out_rs.at[r, 3])

    own_send(0)
    w_own_send(0)
    own_send(1)
    w_sibling_send(0)
    w_sibling_send(1)
    adapters_pick()
    places = request_places()

    def step0():
        w_own_send(1)
        w_first(0)
        w_sibling_send(2)
        w_sibling_send(3)

    def step1():
        w_second(0)
        w_own_send(2)
        w_first(1)
        down_compact(places)

    def step2():
        w_third(0)
        w_second(1)
        w_own_send(3)
        w_first(2)
        up_compact(places)

    def step3():
        w_third(1)
        w_second(2)
        w_ready(0)
        tok_copy.wait()
        base(0, 0)

    def step4():
        w_third(2)
        w_first(3)
        w_ready(1)
        base(0, 1)

    def step5():
        w_second(3)
        adapters_forward(0, dc)
        w_ready(2)
        base(0, 2)

    def step6():
        w_third(3)
        adapters_forward(1, uc)

    def step7():
        w_ready(3)
        base(0, 3)
        adapters_ready(0, dc)
        for k in range(NK):
            low_rank(0, k)
        codes_send(0)
        base(1, 0)
        low_rank(1, 0)
        adapters_ready(1, uc)
        finish(0)

    def step8():
        base(1, 1)
        low_rank(1, 1)
        base(1, 2)
        low_rank(1, 2)

    def step9():
        low_rank(1, 3)
        codes_send(1)
        base(1, 3)
        finish(1)

    steps = [step0, step1, step2, step3, step4, step5, step6, step7, step8, step9]
    for p in range(PIECES + 2):
        if p + 2 < PIECES:
            own_send(p + 2)
        if p < PIECES:
            tok_first(p)
        if 0 <= p - 1 < PIECES:
            tok_second(p - 1)
        if 0 <= p - 2 < PIECES:
            tok_third(p - 2)
        steps[p]()
    for r in range(HALVES):
        out_arrived(r)
    for copy in sends:
        copy.wait_send()


def local(tokens, weight, down, up, lengths, request_adapter_id, adapter_storage_slot):
    dma = pltpu.SemaphoreType.DMA
    any_space = pl.BlockSpec(memory_space=pl.ANY)
    smem = pl.BlockSpec(memory_space=pltpu.SMEM)
    slots = GROUPS * CAP
    out = pl.pallas_call(
        kernel,
        out_shape=jax.ShapeDtypeStruct((2, SOURCES, 2, SHARD, COLS), BF16),
        in_specs=[any_space] * 4 + [smem] * 3,
        out_specs=any_space,
        scratch_shapes=[
            pltpu.VMEM((SOURCES, SHARD, WIDTH), BF16),
            pltpu.VMEM((4, WIDTH, COLS), BF16),
            pltpu.VMEM((OWNED, 2, WIDTH), BF16),
            pltpu.VMEM((OWNED, RANK, COLS), BF16),
            pltpu.VMEM((slots, 2, WIDTH), BF16),
            pltpu.VMEM((slots, RANK, COLS), BF16),
            pltpu.VMEM((slots, 2, WIDTH), BF16),
            pltpu.VMEM((slots, RANK, COLS), BF16),
            pltpu.VMEM((2 * REQUESTS, WIDTH), F32),
            pltpu.VMEM((4, 2 * REQUESTS, WIDTH), BF16),
            pltpu.VMEM((4, REQUESTS, RANK, COLS), BF16),
            pltpu.VMEM((HALVES, 4, HROWS, COLS), F32),
            pltpu.VMEM((HALVES, 8 * REQUESTS, HROWS), F32),
            pltpu.VMEM((HALVES, SOURCES, 8, HROWS), F32),
            pltpu.VMEM((HALVES, 4, SOURCES, HALF, COLS), BF16),
            dma((5,)),
            dma((NK,)),
            dma((7, PIECES)),
            dma((7, PIECES)),
            dma((4, NK)),
            dma((4, NK)),
            dma((NK,)),
            dma((NK,)),
            dma((4, NK)),
            dma((4, NK)),
            dma((2, 4)),
            dma((2, 4)),
            dma((2, 3)),
            dma((2, 4)),
            dma((HALVES, 7)),
            dma((HALVES, 7)),
            dma((HALVES, 4)),
            dma((HALVES, 4)),
        ],
        compiler_params=pltpu.CompilerParams(
            collective_id=0, has_side_effects=True, vmem_limit_bytes=60 * 1024 * 1024
        ),
    )(tokens, weight, down, up, lengths, request_adapter_id, adapter_storage_slot)
    return out.reshape(2 * SOURCES * 2 * SHARD, COLS)


def solution(mesh):
    placed = (
        P(("group", "tp"), None),
        P(None, "tp"),
        P("group", "tp", None),
        P("group", None, "tp"),
        P(),
        P(),
        P(),
    )
    return jax.shard_map(
        local, mesh=mesh, in_specs=placed, out_specs=P("group", "tp"), check_vma=False
    )
```

```python
import jax
import jax.numpy as jnp
from jax import lax
from jax.experimental import pallas as pl
from jax.experimental.pallas import tpu as pltpu
from jax.sharding import PartitionSpec as P

MESH = pl.DeviceIdType.MESH
F32 = jnp.float32
BF16 = jnp.bfloat16

CAP = 6
GROUPS = 4
REQUESTS = 16
RANK = 64
WIDTH = 8192
COLS = 256
SHARD = 64
PART = (48, 16)
START = (0, 48)
PARTS = len(PART)
LANES = 128
HALVES = COLS // LANES
SOURCES = 8
NK = 4
KC = WIDTH // NK
WC = KC // 4
PIECES = PARTS * NK
CHUNKS = HALVES * NK
OWNED = 128
W_FAR_DIRECT = (6, 7)

LEFT, RIGHT, FAR, ACROSS, ACROSS_LEFT, ACROSS_RIGHT, ACROSS_FAR = range(7)


def kernel(
    tok_hbm, w_hbm, down_hbm, up_hbm, len_ref, rid_ref, slot_ref, out_hbm,
    tok, wbuf, dloc, uloc, dsend, usend, drecv, urecv, dtmp, dc, uc,
    acc0, acc1, part0, part1, shr0, shr1, spread0, spread1, ost0, ost1,
    loc_sem, own_sem, tok_ss, tok_rs, w_ss, w_rs, ws_ss, ws_rs, wf_ss, wf_rs,
    ad_ss, ad_rs, cp_ss, cp_rs, sh_ss, sh_rs, out_ss, out_rs,
):
    acc, part, shr = (acc0, acc1), (part0, part1), (shr0, shr1)
    spread, ost = (spread0, spread1), (ost0, ost1)
    g = lax.axis_index("group")
    tp = lax.axis_index("tp")
    z = tp // 8
    x = (tp // 2) % 4
    c = tp % 2
    side = z // 2
    bit = z % 2
    z_across = 2 * side + 1 - bit
    z_partner = 3 - z

    def device(zz, xx, cc, gg=None):
        return (g if gg is None else gg, (zz * 4 + xx) * 2 + cc)

    left, right, far = (x + 3) % 4, (x + 1) % 4, (x + 2) % 4
    to_left, to_right = device(z, left, c), device(z, right, c)
    to_across = device(z_across, x, c)
    to_sibling = device(z, x, 1 - c)
    to_partner = device(z_partner, x, c)
    to_partner_other = device(z_partner, x, 1 - c)

    sends = []

    def send(src, dst, ss, rs, dev):
        copy = pltpu.make_async_remote_copy(
            src_ref=src, dst_ref=dst, send_sem=ss, recv_sem=rs, device_id=dev, device_id_type=MESH
        )
        copy.start()
        sends.append(copy)

    waited = set()

    def arrived(key, dst, rs):
        if key not in waited:
            waited.add(key)
            pltpu.make_async_copy(dst, dst, rs).wait()

    def once(key, copy):
        if key not in waited:
            waited.add(key)
            copy.wait()

    down_copy = pltpu.make_async_copy(down_hbm, dloc, loc_sem.at[0])
    up_copy = pltpu.make_async_copy(up_hbm, uloc, loc_sem.at[1])
    mine = bit * 4 + x
    tok_copy = pltpu.make_async_copy(tok_hbm, tok.at[mine], loc_sem.at[2])
    def w_at(m, i, start, rows):
        h, k = divmod(i, NK)
        return wbuf.at[h, pl.ds(k * KC + start, rows), pl.ds(m * LANES, LANES)]

    def w_own_at(i, start, rows):
        h, k = divmod(i, NK)
        return w_hbm.at[pl.ds(k * KC + start, rows), pl.ds(h * LANES, LANES)]

    w_copies = [
        pltpu.make_async_copy(w_own_at(i, 0, KC), w_at(0, i, 0, KC), own_sem.at[i])
        for i in range(CHUNKS)
    ]
    down_copy.start()
    up_copy.start()
    tok_copy.start()
    for copy in w_copies:
        copy.start()

    peers = [device(z, xx, c) for xx in (left, right, far)]
    peers += [device(z_across, xx, c) for xx in (x, left, right, far)]
    near = list(peers)
    peers += [to_sibling, to_partner, to_partner_other]
    peers += [device(z, x, c, (g + d) % GROUPS) for d in (1, 2, 3)]
    barrier = pltpu.get_barrier_semaphore()
    for dev in peers:
        pl.semaphore_signal(barrier, inc=1, device_id=dev, device_id_type=MESH)
    pl.semaphore_wait(barrier, len(peers))

    def at(source, p):
        r, k = divmod(p, NK)
        return tok.at[source, pl.ds(START[r], PART[r]), pl.ds(k * KC, KC)]

    def tok_send(source, p, n, cls, dev):
        send(at(source, p), at(source, p), tok_ss.at[n, p], tok_rs.at[cls, p], dev)

    s_left, s_right, s_far = bit * 4 + left, bit * 4 + right, bit * 4 + far
    other = (1 - bit) * 4
    a_mine, a_left, a_right, a_far = other + x, other + left, other + right, other + far

    def across_first(p):
        return p % 2 == 0

    def relay_right(p):
        return (p // 2) % 2 == 0

    sources = {
        LEFT: s_left, RIGHT: s_right, FAR: s_far, ACROSS: a_mine,
        ACROSS_LEFT: a_left, ACROSS_RIGHT: a_right, ACROSS_FAR: a_far,
    }

    def tok_arrived(cls, p):
        arrived(("tok", cls, p), at(sources[cls], p), tok_rs.at[cls, p])

    def own_piece(p):
        r, k = divmod(p, NK)
        return tok_hbm.at[pl.ds(START[r], PART[r]), pl.ds(k * KC, KC)]

    def own_across(p):
        send(own_piece(p), at(mine, p), tok_ss.at[0, p], tok_rs.at[ACROSS, p], to_across)

    def own_sides(p):
        send(own_piece(p), at(mine, p), tok_ss.at[1, p], tok_rs.at[LEFT, p], to_right)
        send(own_piece(p), at(mine, p), tok_ss.at[2, p], tok_rs.at[RIGHT, p], to_left)

    def pass_across(p):
        tok_arrived(ACROSS, p)
        tok_send(a_mine, p, 3, ACROSS_LEFT, to_right)
        tok_send(a_mine, p, 4, ACROSS_RIGHT, to_left)

    def pass_left(p):
        tok_arrived(LEFT, p)
        if relay_right(p):
            tok_send(s_left, p, 5, FAR, to_right)
        if not across_first(p):
            tok_send(s_left, p, 3, ACROSS_LEFT, to_across)

    def pass_right(p):
        tok_arrived(RIGHT, p)
        if not relay_right(p):
            tok_send(s_right, p, 5, FAR, to_left)
        if not across_first(p):
            tok_send(s_right, p, 4, ACROSS_RIGHT, to_across)

    def pass_far(p):
        tok_arrived(FAR, p)
        tok_send(s_far, p, 6, ACROSS_FAR, to_across)

    def pass_across_left(p):
        tok_arrived(ACROSS_LEFT, p)
        tok_send(a_left, p, 6, ACROSS_FAR, to_right)

    def pass_across_right(p):
        tok_arrived(ACROSS_RIGHT, p)
        tok_send(a_right, p, 6, ACROSS_FAR, to_left)

    def tok_ready(r, k):
        once("own tokens", tok_copy)
        for cls in sources:
            tok_arrived(cls, r * NK + k)

    g_next, g_prev, g_far = (g + 1) % GROUPS, (g + 3) % GROUPS, (g + 2) % GROUPS
    to_next, to_prev = device(z, x, c, g_next), device(z, x, c, g_prev)
    w_quarters = (g, g_prev, g_far, g_next)

    def w_own(i):
        src, dst = w_own_at(i, g * WC, WC), w_at(2, i, g * WC, WC)
        send(src, dst, w_ss.at[0, i], w_rs.at[0, i], to_partner)

    def w_own_far(i):
        src, dst = w_own_at(i, g_far * WC, WC), w_at(2, i, g_far * WC, WC)
        send(src, dst, w_ss.at[3, i], w_rs.at[2, i], to_partner)

    def w_sibling(i):
        src, dst = w_own_at(i, 0, KC), w_at(1, i, 0, KC)
        send(src, dst, ws_ss.at[i], ws_rs.at[i], to_sibling)

    def w_arrived(cls, i):
        arrived(("w", cls, i), w_at(2, i, w_quarters[cls] * WC, WC), w_rs.at[cls, i])

    def w_forward(i, cls):
        start = w_quarters[cls] * WC
        src, dst = w_at(2, i, start, WC), w_at(3, i, start, WC)
        send(src, dst, wf_ss.at[cls, i], wf_rs.at[cls, i], to_sibling)

    def w_send(i, q, n, cls, dev):
        ref = w_at(2, i, q * WC, WC)
        send(ref, ref, w_ss.at[n, i], w_rs.at[cls, i], dev)

    def w_pass(i):
        w_arrived(0, i)
        w_send(i, g, 1, 1, to_next)
        w_send(i, g, 2, 3, to_prev)
        w_forward(i, 0)

    def w_pass_prev(i):
        w_arrived(1, i)
        if i not in W_FAR_DIRECT and i % 2 == 0:
            w_send(i, g_prev, 3, 2, to_next)
        w_forward(i, 1)

    def w_pass_next(i):
        w_arrived(3, i)
        if i not in W_FAR_DIRECT and i % 2 == 1:
            w_send(i, g_next, 3, 2, to_prev)
        w_forward(i, 3)

    def w_pass_far(i):
        w_arrived(2, i)
        w_forward(i, 2)

    def w_ready(i):
        once(("own w", i), w_copies[i])
        arrived(("sibling w", i), w_at(1, i, 0, KC), ws_rs.at[i])
        for cls, q in enumerate(w_quarters):
            arrived(("other w", cls, i), w_at(3, i, q * WC, WC), wf_rs.at[cls, i])

    def picked_places():
        picked = []
        for dest in range(GROUPS):
            index = [jnp.int32(0)] * CAP
            count = jnp.int32(0)
            for j in range(REQUESTS):
                slot = slot_ref[rid_ref[dest, j]]
                is_mine = slot // OWNED == g
                local = slot % OWNED
                for p in range(min(CAP, j + 1)):
                    index[p] = jnp.where(is_mine & (count == p), local, index[p])
                count = count + is_mine.astype(jnp.int32)
            picked += index
        return picked

    def adapters_send(n, table, picks, gets):
        for p in range(GROUPS * CAP):
            picks[p] = table[picked[p]]
        for d in (1, 3, 2):
            rows = pl.ds(((g + d) % GROUPS) * CAP, CAP)
            dev = device(z, x, c, (g + d) % GROUPS)
            send(picks.at[rows], gets.at[pl.ds(g * CAP, CAP)], ad_ss.at[n, d], ad_rs.at[n, d], dev)
        rows = pl.ds(g * CAP, CAP)
        pltpu.make_async_copy(picks.at[rows], gets.at[rows], ad_ss.at[n, 0]).start()

    def down_pick():
        down_copy.wait()
        adapters_send(0, dloc, dsend, drecv)

    def up_pick():
        up_copy.wait()
        adapters_send(1, uloc, usend, urecv)

    def request_places():
        places = []
        counts = [jnp.int32(0)] * GROUPS
        for j in range(REQUESTS):
            owner = slot_ref[rid_ref[g, j]] // OWNED
            place = jnp.int32(0)
            for o in range(GROUPS):
                hit = owner == o
                place = place + jnp.where(hit, o * CAP + counts[o], 0)
                counts[o] = counts[o] + hit.astype(jnp.int32)
            places.append(place)
        return places

    def adapters_arrived(n, ref, src):
        rows = pl.ds(g * CAP, CAP)
        pltpu.make_async_copy(src.at[rows], ref.at[rows], ad_ss.at[n, 0]).wait()
        for d in (1, 2, 3):
            rows = pl.ds(((g + 4 - d) % GROUPS) * CAP, CAP)
            arrived(("picked", n, d), ref.at[rows], ad_rs.at[n, d])

    def adapters_share(n, ref):
        send(ref.at[0], ref.at[2], cp_ss.at[n, 0], cp_rs.at[n, 2], to_partner)
        send(ref.at[0], ref.at[1], cp_ss.at[n, 1], cp_rs.at[n, 1], to_sibling)

    def down_compact():
        adapters_arrived(0, drecv, dsend)
        for j in range(REQUESTS):
            dtmp[2 * j : 2 * j + 2, :] = drecv[places[j]].astype(F32)
        dc[0] = dtmp[...].astype(BF16)
        adapters_share(0, dc)

    def up_compact():
        adapters_arrived(1, urecv, usend)
        for j in range(REQUESTS):
            uc[0, j] = urecv[places[j]]
        adapters_share(1, uc)

    def down_forward():
        adapters_forward(0, dc)

    def up_forward():
        adapters_forward(1, uc)

    def adapters_forward(n, ref):
        arrived(("adapters", n, 2), ref.at[2], cp_rs.at[n, 2])
        send(ref.at[2], ref.at[3], cp_ss.at[n, 2], cp_rs.at[n, 3], to_sibling)

    def adapters_ready(n, ref):
        arrived(("adapters", n, 1), ref.at[1], cp_rs.at[n, 1])
        arrived(("adapters", n, 3), ref.at[3], cp_rs.at[n, 3])

    begun = set()

    def add(key, ref, term):
        if key in begun:
            ref[...] += term
        else:
            begun.add(key)
            ref[...] = term

    def token_block(r, k):
        rows = tok[:, START[r] : START[r] + PART[r], k * KC : (k + 1) * KC]
        return rows.reshape(SOURCES * PART[r], KC)

    def base(r, k, h):
        tok_ready(r, k)
        w_ready(h * NK + k)
        weight = wbuf[h, k * KC : (k + 1) * KC, :]
        term = jnp.dot(token_block(r, k), weight, preferred_element_type=F32)
        add(("base", r, h), acc[r].at[h], term)

    def low_rank(r, k):
        tok_ready(r, k)
        adapters_ready(0, dc)
        rows = dc[:, :, k * KC : (k + 1) * KC].reshape(4 * 2 * REQUESTS, KC)
        term = lax.dot_general(
            rows, token_block(r, k), (((1,), (1,)), ((), ())), preferred_element_type=F32
        )
        add(("low rank", r), part[r], term)

    ends = []
    total = jnp.int32(0)
    for j in range(REQUESTS):
        total = total + len_ref[g, j]
        ends.append(total)

    def request_of(row, r):
        source = jnp.zeros(row.shape, jnp.int32)
        for n in range(1, SOURCES):
            source = source + jnp.where(row >= n * PART[r], 1, 0)
        position = side * 1024 + source * 128 + c * SHARD + START[r] + row - source * PART[r]
        request = jnp.zeros(row.shape, jnp.int32)
        for j in range(REQUESTS):
            request = request + jnp.where(position >= ends[j], 1, 0)
        return request

    z_low = jnp.minimum(z, z_partner)
    quad = z_low * 4 + x

    def codes_send(r):
        shape = (8 * REQUESTS, SOURCES * PART[r])
        row = lax.broadcasted_iota(jnp.int32, shape, 0)
        request = request_of(lax.broadcasted_iota(jnp.int32, shape, 1), r)
        masked = jnp.where(request == (row % 32) // 2, part[r][...], 0.0).astype(BF16)
        lane = lax.broadcasted_iota(jnp.int32, (16, 128), 1)
        member = lane // 32
        high = jnp.where(z == z_low, member // 2, 1 - member // 2)
        core = jnp.where(c == 0, member % 2, 1 - member % 2)
        place = high * 4 + core * 2 + lane % 2
        pick = jnp.where(place == lax.broadcasted_iota(jnp.int32, (16, 128), 0), 1.0, 0.0)
        codes = jnp.dot(pick.astype(BF16), masked, preferred_element_type=F32)
        shr[r][quad] = codes[:8]
        for n, dev in enumerate(near):
            cls = (RIGHT, LEFT, FAR, ACROSS, ACROSS_RIGHT, ACROSS_LEFT, ACROSS_FAR)[n]
            ref = shr[r].at[quad]
            send(ref, ref, sh_ss.at[r, n], sh_rs.at[r, cls], dev)

    def out_piece(zz, cc, r, h):
        rows, lanes = pl.ds(START[r], PART[r]), pl.ds(h * LANES, LANES)
        return out_hbm.at[zz // 2, :, cc, rows, lanes]

    def out_local(r, h):
        sem = loc_sem.at[3 + r * HALVES + h]
        return pltpu.make_async_copy(ost[r].at[h, 0], out_piece(z, c, r, h), sem)

    def codes_spread(r):
        z_other_low = 1 - z_low
        quad_low, quad_other = z_low * 4, z_other_low * 4
        for cls, q in (
            (LEFT, quad_low + left), (RIGHT, quad_low + right), (FAR, quad_low + far),
            (ACROSS, quad_other + x), (ACROSS_LEFT, quad_other + left),
            (ACROSS_RIGHT, quad_other + right), (ACROSS_FAR, quad_other + far),
        ):
            arrived(("codes", r, cls), shr[r].at[q], sh_rs.at[r, cls])
        place = lax.broadcasted_iota(jnp.int32, (RANK, 128), 0)
        lane = lax.broadcasted_iota(jnp.int32, (RANK, 128), 1) % RANK
        low, xx, rest = place // 32, (place // 8) % 4, place % 8
        zz = jnp.where(rest // 4 == 0, low, 3 - low)
        rank = zz * 16 + xx * 4 + rest % 4
        order = jnp.where(rank == lane, 1.0, 0.0).astype(BF16)
        hrows = SOURCES * PART[r]
        codes = shr[r][...].reshape(RANK, hrows).astype(BF16)
        codes = lax.dot_general(codes, order, (((0,), (0,)), ((), ())), preferred_element_type=F32)
        request = request_of(lax.broadcasted_iota(jnp.int32, (hrows, 128), 0), r)
        half = lax.broadcasted_iota(jnp.int32, (hrows, 128), 1) // RANK
        request = request - half
        for b in range(REQUESTS // 2):
            block = jnp.where(request == 2 * b, codes, 0.0).astype(BF16)
            spread[r][:, b * 128 : (b + 1) * 128] = block

    def finish(r, h):
        adapters_ready(1, uc)
        lanes = slice(h * LANES, (h + 1) * LANES)
        for pair in (1, 0):
            table = jnp.concatenate(
                [uc[m, :, :, lanes].reshape(REQUESTS * RANK, LANES) for m in (2 * pair, 2 * pair + 1)],
                axis=1,
            )
            update = jnp.dot(spread[r][...], table, preferred_element_type=F32)
            base_sum = acc[r][h, :, pair * 2 * LANES : (pair + 1) * 2 * LANES]
            result = (base_sum + 0.5 * update).astype(BF16)
            for n in (0, 1):
                m = 2 * pair + n
                piece = result[:, n * LANES : (n + 1) * LANES]
                ost[r][h, m] = piece.reshape(SOURCES, PART[r], LANES)
                if m == 0:
                    out_local(r, h).start()
                else:
                    dev = (None, to_sibling, to_partner, to_partner_other)[m]
                    ss, rs = out_ss.at[r, h, m], out_rs.at[r, h, m]
                    send(ost[r].at[h, m], out_piece(z, c, r, h), ss, rs, dev)

    def out_arrived(r, h):
        out_local(r, h).wait()
        for m, (zz, cc) in enumerate(((z, 1 - c), (z_partner, c), (z_partner, 1 - c)), 1):
            arrived(("out", r, h, m), out_piece(zz, cc, r, h), out_rs.at[r, h, m])

    picked = picked_places()
    places = request_places()

    order = [
        (w_own, 4), (w_sibling, 4), (w_own, 6), (own_across, 0), (own_sides, 0), (w_sibling, 0),
        (w_sibling, 1), (w_own_far, 6), (w_own, 0), (w_own_far, 7), (w_sibling, 3), (w_sibling, 7),
        (w_sibling, 2), (w_own, 7), (own_across, 1), (w_own, 5), (w_own, 3), (w_own, 2),
        (own_sides, 1), (own_sides, 2), (own_across, 2), (w_sibling, 6), (w_own, 1), (w_sibling, 5),
        (down_pick,), (own_sides, 3), (own_across, 3), (pass_left, 0), (w_pass, 4), (up_pick,),
        (pass_across, 0), (w_pass_far, 6), (own_across, 4), (pass_left, 1), (pass_right, 1),
        (pass_across, 2), (pass_right, 2), (down_compact,), (w_pass_far, 7), (w_pass, 0),
        (w_pass_prev, 4), (w_pass_next, 4), (pass_left, 3), (pass_right, 3), (pass_across, 4),
        (w_pass, 5), (w_pass, 7), (up_compact,), (pass_across_right, 2), (pass_across_left, 0),
        (own_across, 5), (w_pass, 2), (w_pass_prev, 0), (w_pass_next, 0), (own_across, 6),
        (own_across, 7), (pass_far, 1), (w_pass_far, 4), (w_pass_next, 5), (own_sides, 4),
        (own_sides, 5), (w_pass, 6), (w_pass_prev, 5), (w_pass_next, 7), (own_sides, 6),
        (pass_far, 3), (own_sides, 7), (pass_across_left, 4), (w_pass, 1), (w_pass_prev, 7),
        (w_pass_next, 2), (pass_across, 6), (w_pass, 3), (w_pass_far, 5), (down_forward,),
        (w_pass_prev, 2), (base, 0, 0, 1), (pass_left, 4), (w_pass_far, 0), (low_rank, 0, 2),
        (w_pass_next, 6), (pass_left, 5), (pass_right, 5), (low_rank, 0, 0), (base, 0, 0, 0),
        (base, 0, 1, 1), (w_pass_prev, 6), (pass_right, 6), (w_pass_next, 1), (pass_left, 7),
        (pass_right, 7), (low_rank, 0, 1), (base, 0, 2, 1), (pass_across_right, 6),
        (w_pass_prev, 1), (w_pass_next, 3), (low_rank, 0, 3), (base, 0, 3, 1), (codes_send, 0),
        (base, 1, 0, 1), (pass_far, 7), (low_rank, 1, 0), (up_forward,), (base, 1, 0, 0),
        (pass_far, 5), (base, 1, 2, 1), (low_rank, 1, 2), (w_pass_prev, 3), (codes_spread, 0),
        (w_pass_far, 1), (finish, 0, 1), (w_pass_far, 2), (w_pass_far, 3), (base, 0, 1, 0),
        (base, 1, 3, 1), (low_rank, 1, 3), (base, 0, 2, 0), (base, 0, 3, 0), (finish, 0, 0),
        (low_rank, 1, 1), (codes_send, 1), (base, 1, 1, 0), (base, 1, 1, 1), (base, 1, 3, 0),
        (base, 1, 2, 0), (codes_spread, 1), (finish, 1, 1), (finish, 1, 0),
    ]
    for action, *args in order:
        action(*args)
    for r in range(PARTS):
        for h in range(HALVES):
            out_arrived(r, h)
    for copy in sends:
        copy.wait_send()


def local(tokens, weight, down, up, lengths, request_adapter_id, adapter_storage_slot):
    dma = pltpu.SemaphoreType.DMA
    any_space = pl.BlockSpec(memory_space=pl.ANY)
    smem = pl.BlockSpec(memory_space=pltpu.SMEM)
    slots = GROUPS * CAP
    out = pl.pallas_call(
        kernel,
        out_shape=jax.ShapeDtypeStruct((2, SOURCES, 2, SHARD, COLS), BF16),
        in_specs=[any_space] * 4 + [smem] * 3,
        out_specs=any_space,
        scratch_shapes=[
            pltpu.VMEM((SOURCES, SHARD, WIDTH), BF16),
            pltpu.VMEM((HALVES, WIDTH, 4 * LANES), BF16),
            pltpu.VMEM((OWNED, 2, WIDTH), BF16),
            pltpu.VMEM((OWNED, RANK, COLS), BF16),
            pltpu.VMEM((slots, 2, WIDTH), BF16),
            pltpu.VMEM((slots, RANK, COLS), BF16),
            pltpu.VMEM((slots, 2, WIDTH), BF16),
            pltpu.VMEM((slots, RANK, COLS), BF16),
            pltpu.VMEM((2 * REQUESTS, WIDTH), F32),
            pltpu.VMEM((4, 2 * REQUESTS, WIDTH), BF16),
            pltpu.VMEM((4, REQUESTS, RANK, COLS), BF16),
            *(pltpu.VMEM((HALVES, SOURCES * n, 4 * LANES), F32) for n in PART),
            *(pltpu.VMEM((8 * REQUESTS, SOURCES * n), F32) for n in PART),
            *(pltpu.VMEM((SOURCES, 8, SOURCES * n), F32) for n in PART),
            *(pltpu.VMEM((SOURCES * n, REQUESTS * RANK), BF16) for n in PART),
            *(pltpu.VMEM((HALVES, 4, SOURCES, n, LANES), BF16) for n in PART),
            dma((3 + PARTS * HALVES,)),
            dma((CHUNKS,)),
            dma((7, PIECES)),
            dma((7, PIECES)),
            dma((4, CHUNKS)),
            dma((4, CHUNKS)),
            dma((CHUNKS,)),
            dma((CHUNKS,)),
            dma((4, CHUNKS)),
            dma((4, CHUNKS)),
            dma((2, 4)),
            dma((2, 4)),
            dma((2, 3)),
            dma((2, 4)),
            dma((PARTS, 7)),
            dma((PARTS, 7)),
            dma((PARTS, HALVES, 4)),
            dma((PARTS, HALVES, 4)),
        ],
        compiler_params=pltpu.CompilerParams(
            collective_id=0, has_side_effects=True, vmem_limit_bytes=60 * 1024 * 1024
        ),
    )(tokens, weight, down, up, lengths, request_adapter_id, adapter_storage_slot)
    return out.reshape(2 * SOURCES * 2 * SHARD, COLS)


def solution(mesh):
    placed = (
        P(("group", "tp"), None),
        P(None, "tp"),
        P("group", "tp", None),
        P("group", None, "tp"),
        P(),
        P(),
        P(),
    )
    return jax.shard_map(
        local, mesh=mesh, in_specs=placed, out_specs=P("group", "tp"), check_vma=False
    )
```

```python
import jax
import jax.numpy as jnp
from jax import lax
from jax.experimental import pallas as pl
from jax.experimental.pallas import tpu as pltpu
from jax.sharding import PartitionSpec as P

MESH = pl.DeviceIdType.MESH
F32 = jnp.float32
BF16 = jnp.bfloat16

CAP = 6
GROUPS = 4
REQUESTS = 16
RANK = 64
WIDTH = 8192
COLS = 256
SHARD = 64
PART = (48, 16)
START = (0, 48)
PARTS = len(PART)
LANES = 128
HALVES = COLS // LANES
SOURCES = 8
KCS = (2304, 1792, 2304, 1792)
NK = len(KCS)
KSTART = tuple(sum(KCS[:k]) for k in range(NK))
PIECES = PARTS * NK
CHUNKS = HALVES * NK
OWNED = 128
W_FAR_DIRECT = (6, 7)

LEFT, RIGHT, FAR, ACROSS, ACROSS_LEFT, ACROSS_RIGHT, ACROSS_FAR = range(7)


def kernel(
    tok_hbm, w_hbm, down_hbm, up_hbm, len_ref, rid_ref, slot_ref, out_hbm,
    tok, wbuf, dloc, uloc, dsend, usend, drecv, urecv, dtmp, dc, uc,
    acc0, acc1, part0, part1, shr0, shr1, spread0, spread1, ost0, ost1,
    loc_sem, own_sem, tok_ss, tok_rs, w_ss, w_rs, ws_ss, ws_rs, wf_ss, wf_rs,
    ad_ss, ad_rs, cp_ss, cp_rs, sh_ss, sh_rs, out_ss, out_rs,
):
    acc, part, shr = (acc0, acc1), (part0, part1), (shr0, shr1)
    spread, ost = (spread0, spread1), (ost0, ost1)
    g = lax.axis_index("group")
    tp = lax.axis_index("tp")
    z = tp // 8
    x = (tp // 2) % 4
    c = tp % 2
    side = z // 2
    bit = z % 2
    z_across = 2 * side + 1 - bit
    z_partner = 3 - z

    def device(zz, xx, cc, gg=None):
        return (g if gg is None else gg, (zz * 4 + xx) * 2 + cc)

    left, right, far = (x + 3) % 4, (x + 1) % 4, (x + 2) % 4
    to_left, to_right = device(z, left, c), device(z, right, c)
    to_across = device(z_across, x, c)
    to_sibling = device(z, x, 1 - c)
    to_partner = device(z_partner, x, c)
    to_partner_other = device(z_partner, x, 1 - c)

    sends = []

    def sent():
        for copy in sends:
            copy.wait_send()
        sends.clear()

    def send(src, dst, ss, rs, dev):
        copy = pltpu.make_async_remote_copy(
            src_ref=src, dst_ref=dst, send_sem=ss, recv_sem=rs, device_id=dev, device_id_type=MESH
        )
        copy.start()
        sends.append(copy)

    waited = set()

    def arrived(key, dst, rs):
        if key not in waited:
            waited.add(key)
            pltpu.make_async_copy(dst, dst, rs).wait()

    def once(key, copy):
        if key not in waited:
            waited.add(key)
            copy.wait()

    down_copy = pltpu.make_async_copy(down_hbm, dloc, loc_sem.at[0])
    up_copy = pltpu.make_async_copy(up_hbm, uloc, loc_sem.at[1])
    mine = bit * 4 + x
    tok_copy = pltpu.make_async_copy(tok_hbm, tok.at[mine], loc_sem.at[2])
    def w_rows(k, quarter):
        if quarter is None:
            return pl.ds(KSTART[k], KCS[k])
        return pl.ds(KSTART[k] + quarter * (KCS[k] // 4), KCS[k] // 4)

    def w_at(m, i, quarter=None):
        h, k = divmod(i, NK)
        return wbuf.at[h, w_rows(k, quarter), pl.ds(m * LANES, LANES)]

    def w_own_at(i, quarter=None):
        h, k = divmod(i, NK)
        return w_hbm.at[w_rows(k, quarter), pl.ds(h * LANES, LANES)]

    w_copies = [
        pltpu.make_async_copy(w_own_at(i), w_at(0, i), own_sem.at[i])
        for i in range(CHUNKS)
    ]
    down_copy.start()
    up_copy.start()

    peers = [device(z, xx, c) for xx in (left, right, far)]
    peers += [device(z_across, xx, c) for xx in (x, left, right, far)]
    near = list(peers)
    peers += [to_sibling, to_partner, to_partner_other]
    peers += [device(z, x, c, (g + d) % GROUPS) for d in (1, 2, 3)]
    barrier = pltpu.get_barrier_semaphore()
    for dev in peers:
        pl.semaphore_signal(barrier, inc=1, device_id=dev, device_id_type=MESH)
    pl.semaphore_wait(barrier, len(peers))

    def at(source, p):
        r, k = divmod(p, NK)
        return tok.at[source, pl.ds(START[r], PART[r]), pl.ds(KSTART[k], KCS[k])]

    def tok_send(source, p, n, cls, dev):
        send(at(source, p), at(source, p), tok_ss.at[n, p], tok_rs.at[cls, p], dev)

    s_left, s_right, s_far = bit * 4 + left, bit * 4 + right, bit * 4 + far
    other = (1 - bit) * 4
    a_mine, a_left, a_right, a_far = other + x, other + left, other + right, other + far

    def across_first(p):
        return p % 2 == 0

    def relay_right(p):
        return (p // 2) % 2 == 0

    sources = {
        LEFT: s_left, RIGHT: s_right, FAR: s_far, ACROSS: a_mine,
        ACROSS_LEFT: a_left, ACROSS_RIGHT: a_right, ACROSS_FAR: a_far,
    }

    def tok_arrived(cls, p):
        arrived(("tok", cls, p), at(sources[cls], p), tok_rs.at[cls, p])

    def own_piece(p):
        r, k = divmod(p, NK)
        return tok_hbm.at[pl.ds(START[r], PART[r]), pl.ds(KSTART[k], KCS[k])]

    def own_across(p):
        send(own_piece(p), at(mine, p), tok_ss.at[0, p], tok_rs.at[ACROSS, p], to_across)

    def own_sides(p):
        send(own_piece(p), at(mine, p), tok_ss.at[1, p], tok_rs.at[LEFT, p], to_right)
        send(own_piece(p), at(mine, p), tok_ss.at[2, p], tok_rs.at[RIGHT, p], to_left)

    def pass_across(p):
        tok_arrived(ACROSS, p)
        tok_send(a_mine, p, 3, ACROSS_LEFT, to_right)
        tok_send(a_mine, p, 4, ACROSS_RIGHT, to_left)

    def pass_left(p):
        tok_arrived(LEFT, p)
        if relay_right(p):
            tok_send(s_left, p, 5, FAR, to_right)
        if not across_first(p):
            tok_send(s_left, p, 3, ACROSS_LEFT, to_across)

    def pass_right(p):
        tok_arrived(RIGHT, p)
        if not relay_right(p):
            tok_send(s_right, p, 5, FAR, to_left)
        if not across_first(p):
            tok_send(s_right, p, 4, ACROSS_RIGHT, to_across)

    def pass_far(p):
        tok_arrived(FAR, p)
        tok_send(s_far, p, 6, ACROSS_FAR, to_across)

    def pass_across_left(p):
        tok_arrived(ACROSS_LEFT, p)
        tok_send(a_left, p, 6, ACROSS_FAR, to_right)

    def pass_across_right(p):
        tok_arrived(ACROSS_RIGHT, p)
        tok_send(a_right, p, 6, ACROSS_FAR, to_left)

    def tok_ready(r, k):
        once("own tokens", tok_copy)
        for cls in sources:
            tok_arrived(cls, r * NK + k)

    g_next, g_prev, g_far = (g + 1) % GROUPS, (g + 3) % GROUPS, (g + 2) % GROUPS
    to_next, to_prev = device(z, x, c, g_next), device(z, x, c, g_prev)
    w_quarters = (g, g_prev, g_far, g_next)

    def w_own(i):
        src, dst = w_own_at(i, g), w_at(2, i, g)
        send(src, dst, w_ss.at[0, i], w_rs.at[0, i], to_partner)

    def w_own_far(i):
        src, dst = w_own_at(i, g_far), w_at(2, i, g_far)
        send(src, dst, w_ss.at[3, i], w_rs.at[2, i], to_partner)

    def w_sibling(i):
        src, dst = w_own_at(i), w_at(1, i)
        send(src, dst, ws_ss.at[i], ws_rs.at[i], to_sibling)

    def w_arrived(cls, i):
        arrived(("w", cls, i), w_at(2, i, w_quarters[cls]), w_rs.at[cls, i])

    def w_forward(i, cls):
        src, dst = w_at(2, i, w_quarters[cls]), w_at(3, i, w_quarters[cls])
        send(src, dst, wf_ss.at[cls, i], wf_rs.at[cls, i], to_sibling)

    def w_send(i, q, n, cls, dev):
        ref = w_at(2, i, q)
        send(ref, ref, w_ss.at[n, i], w_rs.at[cls, i], dev)

    def w_pass(i):
        w_arrived(0, i)
        w_send(i, g, 1, 1, to_next)
        w_send(i, g, 2, 3, to_prev)
        w_forward(i, 0)

    def w_pass_prev(i):
        w_arrived(1, i)
        if i not in W_FAR_DIRECT and i % 2 == 0:
            w_send(i, g_prev, 3, 2, to_next)
        w_forward(i, 1)

    def w_pass_next(i):
        w_arrived(3, i)
        if i not in W_FAR_DIRECT and i % 2 == 1:
            w_send(i, g_next, 3, 2, to_prev)
        w_forward(i, 3)

    def w_pass_far(i):
        w_arrived(2, i)
        w_forward(i, 2)

    def w_ready(i):
        once(("own w", i), w_copies[i])
        arrived(("sibling w", i), w_at(1, i), ws_rs.at[i])
        for cls, q in enumerate(w_quarters):
            arrived(("other w", cls, i), w_at(3, i, q), wf_rs.at[cls, i])

    def picked_places():
        picked = []
        for dest in range(GROUPS):
            index = [jnp.int32(0)] * CAP
            count = jnp.int32(0)
            for j in range(REQUESTS):
                slot = slot_ref[rid_ref[dest, j]]
                is_mine = slot // OWNED == g
                local = slot % OWNED
                for p in range(min(CAP, j + 1)):
                    index[p] = jnp.where(is_mine & (count == p), local, index[p])
                count = count + is_mine.astype(jnp.int32)
            picked += index
        return picked

    def adapters_send(n, table, picks, gets):
        for p in range(GROUPS * CAP):
            picks[p] = table[picked[p]]
        for d in (1, 3, 2):
            rows = pl.ds(((g + d) % GROUPS) * CAP, CAP)
            dev = device(z, x, c, (g + d) % GROUPS)
            send(picks.at[rows], gets.at[pl.ds(g * CAP, CAP)], ad_ss.at[n, d], ad_rs.at[n, d], dev)
        rows = pl.ds(g * CAP, CAP)
        pltpu.make_async_copy(picks.at[rows], gets.at[rows], ad_ss.at[n, 0]).start()

    picked = []

    def down_pick():
        picked.extend(picked_places())
        down_copy.wait()
        adapters_send(0, dloc, dsend, drecv)
        tok_copy.start()
        for copy in w_copies:
            copy.start()

    def up_pick():
        up_copy.wait()
        adapters_send(1, uloc, usend, urecv)

    def request_places():
        places = []
        counts = [jnp.int32(0)] * GROUPS
        for j in range(REQUESTS):
            owner = slot_ref[rid_ref[g, j]] // OWNED
            place = jnp.int32(0)
            for o in range(GROUPS):
                hit = owner == o
                place = place + jnp.where(hit, o * CAP + counts[o], 0)
                counts[o] = counts[o] + hit.astype(jnp.int32)
            places.append(place)
        return places

    def adapters_arrived(n, ref, src):
        rows = pl.ds(g * CAP, CAP)
        pltpu.make_async_copy(src.at[rows], ref.at[rows], ad_ss.at[n, 0]).wait()
        for d in (1, 2, 3):
            rows = pl.ds(((g + 4 - d) % GROUPS) * CAP, CAP)
            arrived(("picked", n, d), ref.at[rows], ad_rs.at[n, d])

    def adapters_share(n, ref):
        send(ref.at[0], ref.at[2], cp_ss.at[n, 0], cp_rs.at[n, 2], to_partner)
        send(ref.at[0], ref.at[1], cp_ss.at[n, 1], cp_rs.at[n, 1], to_sibling)

    places = []

    def down_compact():
        places.extend(request_places())
        adapters_arrived(0, drecv, dsend)
        for j in range(REQUESTS):
            dtmp[2 * j : 2 * j + 2, :] = drecv[places[j]].astype(F32)
        dc[0] = dtmp[...].astype(BF16)
        adapters_share(0, dc)

    def up_compact():
        adapters_arrived(1, urecv, usend)
        for j in range(REQUESTS):
            uc[0, j] = urecv[places[j]]
        adapters_share(1, uc)

    def down_forward():
        adapters_forward(0, dc)

    def up_forward():
        adapters_forward(1, uc)

    def adapters_forward(n, ref):
        arrived(("adapters", n, 2), ref.at[2], cp_rs.at[n, 2])
        send(ref.at[2], ref.at[3], cp_ss.at[n, 2], cp_rs.at[n, 3], to_sibling)

    def adapters_ready(n, ref):
        arrived(("adapters", n, 1), ref.at[1], cp_rs.at[n, 1])
        arrived(("adapters", n, 3), ref.at[3], cp_rs.at[n, 3])

    begun = set()

    def add(key, ref, term):
        if key in begun:
            ref[...] += term
        else:
            begun.add(key)
            ref[...] = term

    def token_block(r, k):
        rows = tok[:, START[r] : START[r] + PART[r], KSTART[k] : KSTART[k] + KCS[k]]
        return rows.reshape(SOURCES * PART[r], KCS[k])

    def base(r, k, h):
        tok_ready(r, k)
        w_ready(h * NK + k)
        weight = wbuf[h, KSTART[k] : KSTART[k] + KCS[k], :]
        term = jnp.dot(token_block(r, k), weight, preferred_element_type=F32)
        add(("base", r, h), acc[r].at[h], term)

    def low_rank(r, k):
        tok_ready(r, k)
        adapters_ready(0, dc)
        rows = dc[:, :, KSTART[k] : KSTART[k] + KCS[k]].reshape(8 * REQUESTS, KCS[k])
        term = lax.dot_general(
            rows, token_block(r, k), (((1,), (1,)), ((), ())), preferred_element_type=F32
        )
        add(("low rank", r), part[r], term)

    ends = []
    total = jnp.int32(0)
    for j in range(REQUESTS):
        total = total + len_ref[g, j]
        ends.append(total)

    def request_of(row, r):
        source = jnp.zeros(row.shape, jnp.int32)
        for n in range(1, SOURCES):
            source = source + jnp.where(row >= n * PART[r], 1, 0)
        position = side * 1024 + source * 128 + c * SHARD + START[r] + row - source * PART[r]
        request = jnp.zeros(row.shape, jnp.int32)
        for j in range(REQUESTS):
            request = request + jnp.where(position >= ends[j], 1, 0)
        return request

    z_low = jnp.minimum(z, z_partner)
    quad = z_low * 4 + x

    first_late = []

    def codes_send(r):
        if r == PARTS - 1:
            first_late.append(len(sends))
        shape = (8 * REQUESTS, SOURCES * PART[r])
        row = lax.broadcasted_iota(jnp.int32, shape, 0)
        request = request_of(lax.broadcasted_iota(jnp.int32, shape, 1), r)
        masked = jnp.where(request == (row % 32) // 2, part[r][...], 0.0).astype(BF16)
        lane = lax.broadcasted_iota(jnp.int32, (16, 128), 1)
        member = lane // 32
        high = jnp.where(z == z_low, member // 2, 1 - member // 2)
        core = jnp.where(c == 0, member % 2, 1 - member % 2)
        place = high * 4 + core * 2 + lane % 2
        pick = jnp.where(place == lax.broadcasted_iota(jnp.int32, (16, 128), 0), 1.0, 0.0)
        codes = jnp.dot(pick.astype(BF16), masked, preferred_element_type=F32)
        shr[r][quad] = codes[:8]
        for n, dev in enumerate(near):
            cls = (RIGHT, LEFT, FAR, ACROSS, ACROSS_RIGHT, ACROSS_LEFT, ACROSS_FAR)[n]
            ref = shr[r].at[quad]
            send(ref, ref, sh_ss.at[r, n], sh_rs.at[r, cls], dev)

    def out_piece(zz, cc, r, h):
        rows, lanes = pl.ds(START[r], PART[r]), pl.ds(h * LANES, LANES)
        return out_hbm.at[zz // 2, :, cc, rows, lanes]

    def out_local(r, h):
        sem = loc_sem.at[3 + r * HALVES + h]
        return pltpu.make_async_copy(ost[r].at[h, 0], out_piece(z, c, r, h), sem)

    def codes_spread(r):
        if r == PARTS - 1:
            late = sends[first_late[0] :]
            del sends[first_late[0] :]
            sent()
            sends.extend(late)
        z_other_low = 1 - z_low
        quad_low, quad_other = z_low * 4, z_other_low * 4
        for cls, q in (
            (LEFT, quad_low + left), (RIGHT, quad_low + right), (FAR, quad_low + far),
            (ACROSS, quad_other + x), (ACROSS_LEFT, quad_other + left),
            (ACROSS_RIGHT, quad_other + right), (ACROSS_FAR, quad_other + far),
        ):
            arrived(("codes", r, cls), shr[r].at[q], sh_rs.at[r, cls])
        place = lax.broadcasted_iota(jnp.int32, (RANK, 128), 0)
        lane = lax.broadcasted_iota(jnp.int32, (RANK, 128), 1) % RANK
        low, xx, rest = place // 32, (place // 8) % 4, place % 8
        zz = jnp.where(rest // 4 == 0, low, 3 - low)
        rank = zz * 16 + xx * 4 + rest % 4
        order = jnp.where(rank == lane, 1.0, 0.0).astype(BF16)
        hrows = SOURCES * PART[r]
        codes = shr[r][...].reshape(RANK, hrows).astype(BF16)
        codes = lax.dot_general(codes, order, (((0,), (0,)), ((), ())), preferred_element_type=F32)
        request = request_of(lax.broadcasted_iota(jnp.int32, (hrows, 128), 0), r)
        half = lax.broadcasted_iota(jnp.int32, (hrows, 128), 1) // RANK
        request = request - half
        for b in range(REQUESTS // 2):
            block = jnp.where(request == 2 * b, codes, 0.0).astype(BF16)
            spread[r][:, b * 128 : (b + 1) * 128] = block

    def finish(r, h):
        adapters_ready(1, uc)
        lanes = slice(h * LANES, (h + 1) * LANES)
        for pair in (1, 0):
            table = jnp.concatenate(
                [uc[m, :, :, lanes].reshape(REQUESTS * RANK, LANES) for m in (2 * pair, 2 * pair + 1)],
                axis=1,
            )
            update = jnp.dot(spread[r][...], table, preferred_element_type=F32)
            base_sum = acc[r][h, :, pair * 2 * LANES : (pair + 1) * 2 * LANES]
            result = (base_sum + 0.5 * update).astype(BF16)
            for n in (0, 1):
                m = 2 * pair + n
                piece = result[:, n * LANES : (n + 1) * LANES]
                ost[r][h, m] = piece.reshape(SOURCES, PART[r], LANES)
                if m == 0:
                    out_local(r, h).start()
                else:
                    dev = (None, to_sibling, to_partner, to_partner_other)[m]
                    ss, rs = out_ss.at[r, h, m], out_rs.at[r, h, m]
                    send(ost[r].at[h, m], out_piece(z, c, r, h), ss, rs, dev)

    def out_arrived(r, h):
        out_local(r, h).wait()
        for m, (zz, cc) in enumerate(((z, 1 - c), (z_partner, c), (z_partner, 1 - c)), 1):
            arrived(("out", r, h, m), out_piece(zz, cc, r, h), out_rs.at[r, h, m])

    order = [
        (w_own, 2), (own_sides, 0), (w_own, 1), (w_sibling, 4), (w_own_far, 7), (w_own, 6),
        (w_own, 5), (w_sibling, 1), (w_own, 0), (own_across, 0), (own_across, 1), (w_sibling, 2),
        (w_sibling, 0), (w_sibling, 3), (w_sibling, 5), (w_own, 4), (own_sides, 1), (own_sides, 2),
        (down_pick,), (up_pick,), (w_sibling, 7), (own_across, 2), (w_sibling, 6), (w_own_far, 6),
        (w_own, 7), (own_sides, 3), (pass_left, 0), (w_own, 3), (own_across, 3), (pass_across, 0),
        (w_pass_far, 7), (pass_left, 1), (pass_right, 1), (w_pass, 6), (down_compact,),
        (pass_right, 2), (pass_across, 2), (w_pass, 5), (pass_left, 3), (pass_right, 3),
        (w_pass, 0), (up_compact,), (w_pass, 4), (w_pass_far, 6), (w_pass_prev, 6),
        (w_pass_next, 6), (w_pass, 2), (own_across, 4), (own_across, 5), (w_pass_prev, 5),
        (w_pass_next, 5), (pass_across_left, 0), (w_pass, 7), (own_across, 6), (own_across, 7),
        (w_pass, 3), (w_pass_prev, 0), (w_pass_next, 0), (pass_far, 1), (own_sides, 4),
        (pass_across_right, 2), (w_pass_prev, 4), (w_pass_next, 4), (own_sides, 5), (own_sides, 6),
        (pass_across, 4), (pass_far, 3), (w_pass_prev, 2), (w_pass_next, 2), (own_sides, 7),
        (pass_across, 6), (w_pass_prev, 7), (w_pass_far, 5), (down_forward,), (w_pass_prev, 3),
        (w_pass_next, 7), (w_pass, 1), (low_rank, 0, 0), (base, 0, 2, 1), (base, 0, 1, 1),
        (pass_right, 5), (low_rank, 0, 2), (pass_left, 5), (w_pass_far, 0), (w_pass_next, 3),
        (low_rank, 0, 1), (pass_right, 6), (pass_left, 4), (w_pass_next, 1), (base, 0, 0, 0),
        (low_rank, 0, 3), (pass_across_left, 4), (w_pass_far, 4), (codes_send, 0), (pass_left, 7),
        (pass_right, 7), (base, 0, 3, 1), (w_pass_far, 3), (base, 0, 0, 1), (pass_across_right, 6),
        (w_pass_far, 2), (up_forward,), (pass_far, 5), (base, 0, 3, 0), (w_pass_far, 1),
        (codes_spread, 0), (base, 0, 2, 0), (pass_far, 7), (w_pass_prev, 1), (finish, 0, 1),
        (base, 1, 1, 1), (low_rank, 1, 2), (base, 1, 0, 0), (low_rank, 1, 1), (base, 1, 1, 0),
        (base, 0, 1, 0), (low_rank, 1, 0), (base, 1, 3, 0), (low_rank, 1, 3), (codes_send, 1),
        (finish, 0, 0), (base, 1, 3, 1), (base, 1, 0, 1), (base, 1, 2, 1), (base, 1, 2, 0),
        (codes_spread, 1), (finish, 1, 0), (finish, 1, 1),
    ]
    for action, *args in order:
        action(*args)
    for r in range(PARTS):
        for h in range(HALVES):
            out_arrived(r, h)
    sent()


def local(tokens, weight, down, up, lengths, request_adapter_id, adapter_storage_slot):
    dma = pltpu.SemaphoreType.DMA
    any_space = pl.BlockSpec(memory_space=pl.ANY)
    smem = pl.BlockSpec(memory_space=pltpu.SMEM)
    slots = GROUPS * CAP
    out = pl.pallas_call(
        kernel,
        out_shape=jax.ShapeDtypeStruct((2, SOURCES, 2, SHARD, COLS), BF16),
        in_specs=[any_space] * 4 + [smem] * 3,
        out_specs=any_space,
        scratch_shapes=[
            pltpu.VMEM((SOURCES, SHARD, WIDTH), BF16),
            pltpu.VMEM((HALVES, WIDTH, 4 * LANES), BF16),
            pltpu.VMEM((OWNED, 2, WIDTH), BF16),
            pltpu.VMEM((OWNED, RANK, COLS), BF16),
            pltpu.VMEM((slots, 2, WIDTH), BF16),
            pltpu.VMEM((slots, RANK, COLS), BF16),
            pltpu.VMEM((slots, 2, WIDTH), BF16),
            pltpu.VMEM((slots, RANK, COLS), BF16),
            pltpu.VMEM((2 * REQUESTS, WIDTH), F32),
            pltpu.VMEM((4, 2 * REQUESTS, WIDTH), BF16),
            pltpu.VMEM((4, REQUESTS, RANK, COLS), BF16),
            *(pltpu.VMEM((HALVES, SOURCES * n, 4 * LANES), F32) for n in PART),
            *(pltpu.VMEM((8 * REQUESTS, SOURCES * n), F32) for n in PART),
            *(pltpu.VMEM((SOURCES, 8, SOURCES * n), F32) for n in PART),
            *(pltpu.VMEM((SOURCES * n, REQUESTS * RANK), BF16) for n in PART),
            *(pltpu.VMEM((HALVES, 4, SOURCES, n, LANES), BF16) for n in PART),
            dma((3 + PARTS * HALVES,)),
            dma((CHUNKS,)),
            dma((7, PIECES)),
            dma((7, PIECES)),
            dma((4, CHUNKS)),
            dma((4, CHUNKS)),
            dma((CHUNKS,)),
            dma((CHUNKS,)),
            dma((4, CHUNKS)),
            dma((4, CHUNKS)),
            dma((2, 4)),
            dma((2, 4)),
            dma((2, 3)),
            dma((2, 4)),
            dma((PARTS, 7)),
            dma((PARTS, 7)),
            dma((PARTS, HALVES, 4)),
            dma((PARTS, HALVES, 4)),
        ],
        compiler_params=pltpu.CompilerParams(
            collective_id=0, has_side_effects=True, vmem_limit_bytes=60 * 1024 * 1024
        ),
    )(tokens, weight, down, up, lengths, request_adapter_id, adapter_storage_slot)
    return out.reshape(2 * SOURCES * 2 * SHARD, COLS)


def solution(mesh):
    placed = (
        P(("group", "tp"), None),
        P(None, "tp"),
        P("group", "tp", None),
        P("group", None, "tp"),
        P(),
        P(),
        P(),
    )
    return jax.shard_map(
        local, mesh=mesh, in_specs=placed, out_specs=P("group", "tp"), check_vma=False
    )
```

```python
import jax
import jax.numpy as jnp
from jax import lax
from jax.experimental import pallas as pl
from jax.experimental.pallas import tpu as pltpu
from jax.sharding import PartitionSpec as P

MESH = pl.DeviceIdType.MESH
F32 = jnp.float32
BF16 = jnp.bfloat16

CAP = 6
GROUPS = 4
REQUESTS = 16
RANK = 64
WIDTH = 8192
COLS = 256
SHARD = 64
PART = (48, 16)
START = (0, 48)
PARTS = len(PART)
LANES = 128
HALVES = COLS // LANES
SOURCES = 8
KCS = (2176, 1920, 2176, 1920)
NK = len(KCS)
KSTART = tuple(sum(KCS[:k]) for k in range(NK))
PIECES = PARTS * NK
CHUNKS = HALVES * NK
OWNED = 128
W_FAR_DIRECT = (6, 7)

LEFT, RIGHT, FAR, ACROSS, ACROSS_LEFT, ACROSS_RIGHT, ACROSS_FAR = range(7)


def kernel(
    tok_hbm, w_hbm, down_hbm, up_hbm, len_ref, rid_ref, slot_ref, out_hbm,
    tok, wbuf, dloc, uloc, dsend, usend, drecv, urecv, dtmp, dc, uc,
    acc0, acc1, part0, part1, shr0, shr1, spread0, spread1, ost0, ost1,
    loc_sem, own_sem, tok_ss, tok_rs, w_ss, w_rs, ws_ss, ws_rs, wf_ss, wf_rs,
    ad_ss, ad_rs, cp_ss, cp_rs, sh_ss, sh_rs, out_ss, out_rs,
):
    acc, part, shr = (acc0, acc1), (part0, part1), (shr0, shr1)
    spread, ost = (spread0, spread1), (ost0, ost1)
    g = lax.axis_index("group")
    tp = lax.axis_index("tp")
    z = tp // 8
    x = (tp // 2) % 4
    c = tp % 2
    side = z // 2
    bit = z % 2
    z_across = 2 * side + 1 - bit
    z_partner = 3 - z

    def device(zz, xx, cc, gg=None):
        return (g if gg is None else gg, (zz * 4 + xx) * 2 + cc)

    left, right, far = (x + 3) % 4, (x + 1) % 4, (x + 2) % 4
    to_left, to_right = device(z, left, c), device(z, right, c)
    to_across = device(z_across, x, c)
    to_sibling = device(z, x, 1 - c)
    to_partner = device(z_partner, x, c)
    to_partner_other = device(z_partner, x, 1 - c)

    sends = []

    def sent():
        for copy in sends:
            copy.wait_send()
        sends.clear()

    def send(src, dst, ss, rs, dev):
        copy = pltpu.make_async_remote_copy(
            src_ref=src, dst_ref=dst, send_sem=ss, recv_sem=rs, device_id=dev, device_id_type=MESH
        )
        copy.start()
        sends.append(copy)

    waited = set()

    def arrived(key, dst, rs):
        if key not in waited:
            waited.add(key)
            pltpu.make_async_copy(dst, dst, rs).wait()

    def once(key, copy):
        if key not in waited:
            waited.add(key)
            copy.wait()

    down_copy = pltpu.make_async_copy(down_hbm, dloc, loc_sem.at[0])
    up_copy = pltpu.make_async_copy(up_hbm, uloc, loc_sem.at[1])
    mine = bit * 4 + x
    tok_copy = pltpu.make_async_copy(tok_hbm, tok.at[mine], loc_sem.at[2])
    def w_rows(k, quarter):
        if quarter is None:
            return pl.ds(KSTART[k], KCS[k])
        return pl.ds(KSTART[k] + quarter * (KCS[k] // 4), KCS[k] // 4)

    def w_at(m, i, quarter=None):
        h, k = divmod(i, NK)
        return wbuf.at[h, w_rows(k, quarter), pl.ds(m * LANES, LANES)]

    def w_own_at(i, quarter=None):
        h, k = divmod(i, NK)
        return w_hbm.at[w_rows(k, quarter), pl.ds(h * LANES, LANES)]

    w_copies = [
        pltpu.make_async_copy(w_own_at(i), w_at(0, i), own_sem.at[i])
        for i in range(CHUNKS)
    ]
    down_copy.start()
    up_copy.start()

    peers = [device(z, xx, c) for xx in (left, right, far)]
    peers += [device(z_across, xx, c) for xx in (x, left, right, far)]
    near = list(peers)
    peers += [to_sibling, to_partner, to_partner_other]
    peers += [device(z, x, c, (g + d) % GROUPS) for d in (1, 2, 3)]
    barrier = pltpu.get_barrier_semaphore()
    for dev in peers:
        pl.semaphore_signal(barrier, inc=1, device_id=dev, device_id_type=MESH)
    pl.semaphore_wait(barrier, len(peers))

    def at(source, p):
        r, k = divmod(p, NK)
        return tok.at[source, pl.ds(START[r], PART[r]), pl.ds(KSTART[k], KCS[k])]

    def tok_send(source, p, n, cls, dev):
        send(at(source, p), at(source, p), tok_ss.at[n, p], tok_rs.at[cls, p], dev)

    s_left, s_right, s_far = bit * 4 + left, bit * 4 + right, bit * 4 + far
    other = (1 - bit) * 4
    a_mine, a_left, a_right, a_far = other + x, other + left, other + right, other + far

    def across_first(p):
        return p % 2 == 0

    def relay_right(p):
        return (p // 2) % 2 == 0

    sources = {
        LEFT: s_left, RIGHT: s_right, FAR: s_far, ACROSS: a_mine,
        ACROSS_LEFT: a_left, ACROSS_RIGHT: a_right, ACROSS_FAR: a_far,
    }

    def tok_arrived(cls, p):
        arrived(("tok", cls, p), at(sources[cls], p), tok_rs.at[cls, p])

    def own_piece(p):
        r, k = divmod(p, NK)
        return tok_hbm.at[pl.ds(START[r], PART[r]), pl.ds(KSTART[k], KCS[k])]

    def own_across(p):
        send(own_piece(p), at(mine, p), tok_ss.at[0, p], tok_rs.at[ACROSS, p], to_across)

    def own_sides(p):
        send(own_piece(p), at(mine, p), tok_ss.at[1, p], tok_rs.at[LEFT, p], to_right)
        send(own_piece(p), at(mine, p), tok_ss.at[2, p], tok_rs.at[RIGHT, p], to_left)

    def pass_across(p):
        tok_arrived(ACROSS, p)
        tok_send(a_mine, p, 3, ACROSS_LEFT, to_right)
        tok_send(a_mine, p, 4, ACROSS_RIGHT, to_left)

    def pass_left(p):
        tok_arrived(LEFT, p)
        if relay_right(p):
            tok_send(s_left, p, 5, FAR, to_right)
        if not across_first(p):
            tok_send(s_left, p, 3, ACROSS_LEFT, to_across)

    def pass_right(p):
        tok_arrived(RIGHT, p)
        if not relay_right(p):
            tok_send(s_right, p, 5, FAR, to_left)
        if not across_first(p):
            tok_send(s_right, p, 4, ACROSS_RIGHT, to_across)

    def pass_far(p):
        tok_arrived(FAR, p)
        tok_send(s_far, p, 6, ACROSS_FAR, to_across)

    def pass_across_left(p):
        tok_arrived(ACROSS_LEFT, p)
        tok_send(a_left, p, 6, ACROSS_FAR, to_right)

    def pass_across_right(p):
        tok_arrived(ACROSS_RIGHT, p)
        tok_send(a_right, p, 6, ACROSS_FAR, to_left)

    def tok_ready(r, k):
        once("own tokens", tok_copy)
        for cls in sources:
            tok_arrived(cls, r * NK + k)

    g_next, g_prev, g_far = (g + 1) % GROUPS, (g + 3) % GROUPS, (g + 2) % GROUPS
    to_next, to_prev = device(z, x, c, g_next), device(z, x, c, g_prev)
    w_quarters = (g, g_prev, g_far, g_next)

    def w_own(i):
        src, dst = w_own_at(i, g), w_at(2, i, g)
        send(src, dst, w_ss.at[0, i], w_rs.at[0, i], to_partner)

    def w_own_far(i):
        src, dst = w_own_at(i, g_far), w_at(2, i, g_far)
        send(src, dst, w_ss.at[3, i], w_rs.at[2, i], to_partner)

    def w_sibling(i):
        src, dst = w_own_at(i), w_at(1, i)
        send(src, dst, ws_ss.at[i], ws_rs.at[i], to_sibling)

    def w_arrived(cls, i):
        arrived(("w", cls, i), w_at(2, i, w_quarters[cls]), w_rs.at[cls, i])

    def w_forward(i, cls):
        src, dst = w_at(2, i, w_quarters[cls]), w_at(3, i, w_quarters[cls])
        send(src, dst, wf_ss.at[cls, i], wf_rs.at[cls, i], to_sibling)

    def w_send(i, q, n, cls, dev):
        ref = w_at(2, i, q)
        send(ref, ref, w_ss.at[n, i], w_rs.at[cls, i], dev)

    def w_pass(i):
        w_arrived(0, i)
        w_send(i, g, 1, 1, to_next)
        w_send(i, g, 2, 3, to_prev)
        w_forward(i, 0)

    def w_pass_prev(i):
        w_arrived(1, i)
        if i not in W_FAR_DIRECT and i % 2 == 0:
            w_send(i, g_prev, 3, 2, to_next)
        w_forward(i, 1)

    def w_pass_next(i):
        w_arrived(3, i)
        if i not in W_FAR_DIRECT and i % 2 == 1:
            w_send(i, g_next, 3, 2, to_prev)
        w_forward(i, 3)

    def w_pass_far(i):
        w_arrived(2, i)
        w_forward(i, 2)

    def w_ready(i):
        once(("own w", i), w_copies[i])
        arrived(("sibling w", i), w_at(1, i), ws_rs.at[i])
        for cls, q in enumerate(w_quarters):
            arrived(("other w", cls, i), w_at(3, i, q), wf_rs.at[cls, i])

    def picked_places():
        picked = []
        for dest in range(GROUPS):
            index = [jnp.int32(0)] * CAP
            count = jnp.int32(0)
            for j in range(REQUESTS):
                slot = slot_ref[rid_ref[dest, j]]
                is_mine = slot // OWNED == g
                local = slot % OWNED
                for p in range(min(CAP, j + 1)):
                    index[p] = jnp.where(is_mine & (count == p), local, index[p])
                count = count + is_mine.astype(jnp.int32)
            picked += index
        return picked

    def adapters_send(n, table, picks, gets):
        for p in range(GROUPS * CAP):
            picks[p] = table[picked[p]]
        for d in (1, 3, 2):
            rows = pl.ds(((g + d) % GROUPS) * CAP, CAP)
            dev = device(z, x, c, (g + d) % GROUPS)
            send(picks.at[rows], gets.at[pl.ds(g * CAP, CAP)], ad_ss.at[n, d], ad_rs.at[n, d], dev)
        rows = pl.ds(g * CAP, CAP)
        pltpu.make_async_copy(picks.at[rows], gets.at[rows], ad_ss.at[n, 0]).start()

    picked = []

    def down_pick():
        picked.extend(picked_places())
        down_copy.wait()
        adapters_send(0, dloc, dsend, drecv)
        tok_copy.start()
        for copy in w_copies:
            copy.start()

    def up_pick():
        up_copy.wait()
        adapters_send(1, uloc, usend, urecv)

    def request_places():
        places = []
        counts = [jnp.int32(0)] * GROUPS
        for j in range(REQUESTS):
            owner = slot_ref[rid_ref[g, j]] // OWNED
            place = jnp.int32(0)
            for o in range(GROUPS):
                hit = owner == o
                place = place + jnp.where(hit, o * CAP + counts[o], 0)
                counts[o] = counts[o] + hit.astype(jnp.int32)
            places.append(place)
        return places

    def adapters_arrived(n, ref, src):
        rows = pl.ds(g * CAP, CAP)
        pltpu.make_async_copy(src.at[rows], ref.at[rows], ad_ss.at[n, 0]).wait()
        for d in (1, 2, 3):
            rows = pl.ds(((g + 4 - d) % GROUPS) * CAP, CAP)
            arrived(("picked", n, d), ref.at[rows], ad_rs.at[n, d])

    def adapters_share(n, ref):
        send(ref.at[0], ref.at[2], cp_ss.at[n, 0], cp_rs.at[n, 2], to_partner)
        send(ref.at[0], ref.at[1], cp_ss.at[n, 1], cp_rs.at[n, 1], to_sibling)

    places = []

    def down_compact():
        places.extend(request_places())
        adapters_arrived(0, drecv, dsend)
        for j in range(REQUESTS):
            dtmp[2 * j : 2 * j + 2, :] = drecv[places[j]].astype(F32)
        dc[0] = dtmp[...].astype(BF16)
        adapters_share(0, dc)

    def up_compact():
        adapters_arrived(1, urecv, usend)
        for j in range(REQUESTS):
            uc[0, j] = urecv[places[j]]
        adapters_share(1, uc)

    def down_forward():
        adapters_forward(0, dc)

    def up_forward():
        adapters_forward(1, uc)

    def adapters_forward(n, ref):
        arrived(("adapters", n, 2), ref.at[2], cp_rs.at[n, 2])
        send(ref.at[2], ref.at[3], cp_ss.at[n, 2], cp_rs.at[n, 3], to_sibling)

    def adapters_ready(n, ref):
        arrived(("adapters", n, 1), ref.at[1], cp_rs.at[n, 1])
        arrived(("adapters", n, 3), ref.at[3], cp_rs.at[n, 3])

    begun = set()

    def add(key, ref, term):
        if key in begun:
            ref[...] += term
        else:
            begun.add(key)
            ref[...] = term

    def token_block(r, k):
        rows = tok[:, START[r] : START[r] + PART[r], KSTART[k] : KSTART[k] + KCS[k]]
        return rows.reshape(SOURCES * PART[r], KCS[k])

    def base(r, k, h):
        tok_ready(r, k)
        w_ready(h * NK + k)
        weight = wbuf[h, KSTART[k] : KSTART[k] + KCS[k], :]
        term = jnp.dot(token_block(r, k), weight, preferred_element_type=F32)
        add(("base", r, h), acc[r].at[h], term)

    def low_rank(r, k):
        tok_ready(r, k)
        adapters_ready(0, dc)
        rows = dc[:, :, KSTART[k] : KSTART[k] + KCS[k]].reshape(8 * REQUESTS, KCS[k])
        term = lax.dot_general(
            rows, token_block(r, k), (((1,), (1,)), ((), ())), preferred_element_type=F32
        )
        add(("low rank", r), part[r], term)

    ends = []
    total = jnp.int32(0)
    for j in range(REQUESTS):
        total = total + len_ref[g, j]
        ends.append(total)

    def request_of(row, r):
        source = jnp.zeros(row.shape, jnp.int32)
        for n in range(1, SOURCES):
            source = source + jnp.where(row >= n * PART[r], 1, 0)
        position = side * 1024 + source * 128 + c * SHARD + START[r] + row - source * PART[r]
        request = jnp.zeros(row.shape, jnp.int32)
        for j in range(REQUESTS):
            request = request + jnp.where(position >= ends[j], 1, 0)
        return request

    z_low = jnp.minimum(z, z_partner)
    quad = z_low * 4 + x

    first_late = []

    def codes_send(r):
        if r == PARTS - 1:
            first_late.append(len(sends))
        shape = (8 * REQUESTS, SOURCES * PART[r])
        row = lax.broadcasted_iota(jnp.int32, shape, 0)
        request = request_of(lax.broadcasted_iota(jnp.int32, shape, 1), r)
        masked = jnp.where(request == (row % 32) // 2, part[r][...], 0.0).astype(BF16)
        lane = lax.broadcasted_iota(jnp.int32, (16, 128), 1)
        member = lane // 32
        high = jnp.where(z == z_low, member // 2, 1 - member // 2)
        core = jnp.where(c == 0, member % 2, 1 - member % 2)
        place = high * 4 + core * 2 + lane % 2
        pick = jnp.where(place == lax.broadcasted_iota(jnp.int32, (16, 128), 0), 1.0, 0.0)
        codes = jnp.dot(pick.astype(BF16), masked, preferred_element_type=F32)
        shr[r][quad] = codes[:8]
        for n, dev in enumerate(near):
            cls = (RIGHT, LEFT, FAR, ACROSS, ACROSS_RIGHT, ACROSS_LEFT, ACROSS_FAR)[n]
            ref = shr[r].at[quad]
            send(ref, ref, sh_ss.at[r, n], sh_rs.at[r, cls], dev)

    def out_piece(zz, cc, r, h):
        rows, lanes = pl.ds(START[r], PART[r]), pl.ds(h * LANES, LANES)
        return out_hbm.at[zz // 2, :, cc, rows, lanes]

    def out_local(r, h):
        sem = loc_sem.at[3 + r * HALVES + h]
        return pltpu.make_async_copy(ost[r].at[h, 0], out_piece(z, c, r, h), sem)

    def codes_spread(r):
        if r == PARTS - 1:
            late = sends[first_late[0] :]
            del sends[first_late[0] :]
            sent()
            sends.extend(late)
        z_other_low = 1 - z_low
        quad_low, quad_other = z_low * 4, z_other_low * 4
        for cls, q in (
            (LEFT, quad_low + left), (RIGHT, quad_low + right), (FAR, quad_low + far),
            (ACROSS, quad_other + x), (ACROSS_LEFT, quad_other + left),
            (ACROSS_RIGHT, quad_other + right), (ACROSS_FAR, quad_other + far),
        ):
            arrived(("codes", r, cls), shr[r].at[q], sh_rs.at[r, cls])
        place = lax.broadcasted_iota(jnp.int32, (RANK, 128), 0)
        lane = lax.broadcasted_iota(jnp.int32, (RANK, 128), 1) % RANK
        low, xx, rest = place // 32, (place // 8) % 4, place % 8
        zz = jnp.where(rest // 4 == 0, low, 3 - low)
        rank = zz * 16 + xx * 4 + rest % 4
        order = jnp.where(rank == lane, 1.0, 0.0).astype(BF16)
        hrows = SOURCES * PART[r]
        codes = shr[r][...].reshape(RANK, hrows).astype(BF16)
        codes = lax.dot_general(codes, order, (((0,), (0,)), ((), ())), preferred_element_type=F32)
        request = request_of(lax.broadcasted_iota(jnp.int32, (hrows, 128), 0), r)
        half = lax.broadcasted_iota(jnp.int32, (hrows, 128), 1) // RANK
        request = request - half
        for b in range(REQUESTS // 2):
            block = jnp.where(request == 2 * b, codes, 0.0).astype(BF16)
            spread[r][:, b * 128 : (b + 1) * 128] = block

    def finish(r, h, pair):
        adapters_ready(1, uc)
        lanes = slice(h * LANES, (h + 1) * LANES)
        table = jnp.concatenate(
            [uc[m, :, :, lanes].reshape(REQUESTS * RANK, LANES) for m in (2 * pair, 2 * pair + 1)],
            axis=1,
        )
        update = jnp.dot(spread[r][...], table, preferred_element_type=F32)
        base_sum = acc[r][h, :, pair * 2 * LANES : (pair + 1) * 2 * LANES]
        result = (base_sum + 0.5 * update).astype(BF16)
        for n in (1, 0):
            m = 2 * pair + n
            piece = result[:, n * LANES : (n + 1) * LANES]
            ost[r][h, m] = piece.reshape(SOURCES, PART[r], LANES)
            if m == 0:
                out_local(r, h).start()
            else:
                dev = (None, to_sibling, to_partner, to_partner_other)[m]
                ss, rs = out_ss.at[r, h, m], out_rs.at[r, h, m]
                send(ost[r].at[h, m], out_piece(z, c, r, h), ss, rs, dev)

    def out_arrived(r, h):
        out_local(r, h).wait()
        for m, (zz, cc) in enumerate(((z, 1 - c), (z_partner, c), (z_partner, 1 - c)), 1):
            arrived(("out", r, h, m), out_piece(zz, cc, r, h), out_rs.at[r, h, m])

    order = [
        (own_sides, 0), (w_own, 1), (own_across, 0), (w_sibling, 1), (w_own_far, 6), (w_sibling, 6),
        (w_sibling, 3), (own_across, 1), (own_across, 2), (w_own, 3), (w_own, 4), (w_sibling, 5),
        (w_own, 0), (w_own, 2), (w_sibling, 4), (w_sibling, 2), (own_sides, 1), (own_sides, 2),
        (down_pick,), (w_pass, 1), (up_pick,), (own_across, 3), (own_sides, 3), (pass_across, 0),
        (w_sibling, 0), (w_own_far, 7), (w_sibling, 7), (pass_left, 0), (w_own, 7), (w_pass_far, 6),
        (w_own, 5), (w_own, 6), (own_across, 4), (pass_left, 1), (pass_right, 1), (down_compact,),
        (w_pass, 0), (pass_right, 2), (w_pass_prev, 1), (pass_across, 2), (w_pass_next, 1),
        (w_pass, 4), (pass_left, 3), (pass_right, 3), (pass_across, 4), (w_pass, 2),
        (w_pass_far, 7), (pass_across_left, 0), (w_pass, 7), (up_compact,), (own_across, 5),
        (w_pass, 3), (own_across, 6), (w_pass_next, 0), (w_pass_prev, 0), (own_across, 7),
        (w_pass_far, 1), (w_pass_prev, 4), (pass_far, 1), (pass_across_right, 2), (own_sides, 4),
        (w_pass_next, 4), (w_pass_prev, 2), (own_sides, 5), (own_sides, 6), (pass_far, 3),
        (w_pass_prev, 7), (w_pass_next, 2), (own_sides, 7), (pass_across_left, 4), (w_pass, 6),
        (w_pass_prev, 3), (w_pass_next, 7), (pass_across, 6), (down_forward,), (w_pass, 5),
        (w_pass_next, 3), (w_pass_far, 0), (low_rank, 0, 0), (pass_left, 4), (low_rank, 0, 2),
        (base, 0, 0, 0), (base, 0, 1, 0), (w_pass_far, 4), (w_pass_next, 6), (pass_left, 5),
        (pass_right, 5), (low_rank, 0, 1), (pass_right, 6), (base, 0, 0, 1), (w_pass_next, 5),
        (pass_left, 7), (pass_right, 7), (w_pass_far, 2), (low_rank, 0, 3), (codes_send, 0),
        (base, 0, 3, 1), (pass_across_right, 6), (base, 0, 2, 0), (w_pass_far, 3), (w_pass_prev, 6),
        (up_forward,), (pass_far, 7), (low_rank, 1, 0), (base, 0, 3, 0), (base, 1, 0, 0),
        (base, 1, 0, 1), (codes_spread, 0), (pass_far, 5), (base, 1, 2, 1), (finish, 0, 0, 1),
        (w_pass_prev, 5), (base, 1, 3, 0), (low_rank, 1, 2), (base, 1, 2, 0), (w_pass_far, 5),
        (low_rank, 1, 3), (base, 1, 3, 1), (base, 0, 2, 1), (low_rank, 1, 1), (codes_send, 1),
        (base, 0, 1, 1), (finish, 0, 1, 1), (base, 1, 1, 1), (base, 1, 1, 0), (finish, 0, 0, 0),
        (finish, 0, 1, 0), (codes_spread, 1), (finish, 1, 1, 1), (finish, 1, 0, 1),
        (finish, 1, 1, 0), (finish, 1, 0, 0),
    ]
    for action, *args in order:
        action(*args)
    for r in range(PARTS):
        for h in range(HALVES):
            out_arrived(r, h)
    sent()


def local(tokens, weight, down, up, lengths, request_adapter_id, adapter_storage_slot):
    dma = pltpu.SemaphoreType.DMA
    any_space = pl.BlockSpec(memory_space=pl.ANY)
    smem = pl.BlockSpec(memory_space=pltpu.SMEM)
    slots = GROUPS * CAP
    out = pl.pallas_call(
        kernel,
        out_shape=jax.ShapeDtypeStruct((2, SOURCES, 2, SHARD, COLS), BF16),
        in_specs=[any_space] * 4 + [smem] * 3,
        out_specs=any_space,
        scratch_shapes=[
            pltpu.VMEM((SOURCES, SHARD, WIDTH), BF16),
            pltpu.VMEM((HALVES, WIDTH, 4 * LANES), BF16),
            pltpu.VMEM((OWNED, 2, WIDTH), BF16),
            pltpu.VMEM((OWNED, RANK, COLS), BF16),
            pltpu.VMEM((slots, 2, WIDTH), BF16),
            pltpu.VMEM((slots, RANK, COLS), BF16),
            pltpu.VMEM((slots, 2, WIDTH), BF16),
            pltpu.VMEM((slots, RANK, COLS), BF16),
            pltpu.VMEM((2 * REQUESTS, WIDTH), F32),
            pltpu.VMEM((4, 2 * REQUESTS, WIDTH), BF16),
            pltpu.VMEM((4, REQUESTS, RANK, COLS), BF16),
            *(pltpu.VMEM((HALVES, SOURCES * n, 4 * LANES), F32) for n in PART),
            *(pltpu.VMEM((8 * REQUESTS, SOURCES * n), F32) for n in PART),
            *(pltpu.VMEM((SOURCES, 8, SOURCES * n), F32) for n in PART),
            *(pltpu.VMEM((SOURCES * n, REQUESTS * RANK), BF16) for n in PART),
            *(pltpu.VMEM((HALVES, 4, SOURCES, n, LANES), BF16) for n in PART),
            dma((3 + PARTS * HALVES,)),
            dma((CHUNKS,)),
            dma((7, PIECES)),
            dma((7, PIECES)),
            dma((4, CHUNKS)),
            dma((4, CHUNKS)),
            dma((CHUNKS,)),
            dma((CHUNKS,)),
            dma((4, CHUNKS)),
            dma((4, CHUNKS)),
            dma((2, 4)),
            dma((2, 4)),
            dma((2, 3)),
            dma((2, 4)),
            dma((PARTS, 7)),
            dma((PARTS, 7)),
            dma((PARTS, HALVES, 4)),
            dma((PARTS, HALVES, 4)),
        ],
        compiler_params=pltpu.CompilerParams(
            collective_id=0, has_side_effects=True, vmem_limit_bytes=60 * 1024 * 1024
        ),
    )(tokens, weight, down, up, lengths, request_adapter_id, adapter_storage_slot)
    return out.reshape(2 * SOURCES * 2 * SHARD, COLS)


def solution(mesh):
    placed = (
        P(("group", "tp"), None),
        P(None, "tp"),
        P("group", "tp", None),
        P("group", None, "tp"),
        P(),
        P(),
        P(),
    )
    return jax.shard_map(
        local, mesh=mesh, in_specs=placed, out_specs=P("group", "tp"), check_vma=False
    )
```

```python
import jax
import jax.numpy as jnp
from jax import lax
from jax.experimental import pallas as pl
from jax.experimental.pallas import tpu as pltpu
from jax.sharding import PartitionSpec as P

MESH = pl.DeviceIdType.MESH
F32 = jnp.float32
BF16 = jnp.bfloat16

CAP = 6
GROUPS = 4
REQUESTS = 16
RANK = 64
WIDTH = 8192
COLS = 256
SHARD = 64
PART = (48, 16)
START = (0, 48)
PARTS = len(PART)
LANES = 128
HALVES = COLS // LANES
SOURCES = 8
KCS = (2176, 1920, 2176, 1920)
NK = len(KCS)
KSTART = tuple(sum(KCS[:k]) for k in range(NK))
PIECES = PARTS * NK
CHUNKS = HALVES * NK
OWNED = 128
W_FAR_DIRECT = (6, 7)

LEFT, RIGHT, FAR, ACROSS, ACROSS_LEFT, ACROSS_RIGHT, ACROSS_FAR = range(7)


def kernel(
    tok_hbm, w_hbm, down_hbm, up_hbm, len_ref, rid_ref, slot_ref, out_hbm,
    tok, wbuf, dloc, uloc, dsend, usend, drecv, urecv, dtmp, dc, uc,
    acc0, acc1, part0, part1, shr0, shr1, spread0, spread1, ost0, ost1,
    rows0, rows1, lanes0, lanes1,
    loc_sem, own_sem, tok_ss, tok_rs, w_ss, w_rs, ws_ss, ws_rs, wf_ss, wf_rs,
    ad_ss, ad_rs, cp_ss, cp_rs, sh_ss, sh_rs, out_ss, out_rs,
):
    acc, part, shr = (acc0, acc1), (part0, part1), (shr0, shr1)
    spread, ost = (spread0, spread1), (ost0, ost1)
    by_lane, by_row = (rows0, rows1), (lanes0, lanes1)
    g = lax.axis_index("group")
    tp = lax.axis_index("tp")
    z = tp // 8
    x = (tp // 2) % 4
    c = tp % 2
    side = z // 2
    bit = z % 2
    z_across = 2 * side + 1 - bit
    z_partner = 3 - z

    def device(zz, xx, cc, gg=None):
        return (g if gg is None else gg, (zz * 4 + xx) * 2 + cc)

    left, right, far = (x + 3) % 4, (x + 1) % 4, (x + 2) % 4
    to_left, to_right = device(z, left, c), device(z, right, c)
    to_across = device(z_across, x, c)
    to_sibling = device(z, x, 1 - c)
    to_partner = device(z_partner, x, c)
    to_partner_other = device(z_partner, x, 1 - c)

    sends = []

    def sent():
        for copy in sends:
            copy.wait_send()
        sends.clear()

    def send(src, dst, ss, rs, dev):
        copy = pltpu.make_async_remote_copy(
            src_ref=src, dst_ref=dst, send_sem=ss, recv_sem=rs, device_id=dev, device_id_type=MESH
        )
        copy.start()
        sends.append(copy)

    waited = set()

    def arrived(key, dst, rs):
        if key not in waited:
            waited.add(key)
            pltpu.make_async_copy(dst, dst, rs).wait()

    def once(key, copy):
        if key not in waited:
            waited.add(key)
            copy.wait()

    down_copy = pltpu.make_async_copy(down_hbm, dloc, loc_sem.at[0])
    up_copy = pltpu.make_async_copy(up_hbm, uloc, loc_sem.at[1])
    mine = bit * 4 + x
    tok_copy = pltpu.make_async_copy(tok_hbm, tok.at[mine], loc_sem.at[2])
    def w_rows(k, quarter):
        if quarter is None:
            return pl.ds(KSTART[k], KCS[k])
        return pl.ds(KSTART[k] + quarter * (KCS[k] // 4), KCS[k] // 4)

    def w_at(m, i, quarter=None):
        h, k = divmod(i, NK)
        return wbuf.at[h, w_rows(k, quarter), pl.ds(m * LANES, LANES)]

    def w_own_at(i, quarter=None):
        h, k = divmod(i, NK)
        return w_hbm.at[w_rows(k, quarter), pl.ds(h * LANES, LANES)]

    w_copies = [
        pltpu.make_async_copy(w_own_at(i), w_at(0, i), own_sem.at[i])
        for i in range(CHUNKS)
    ]
    down_copy.start()
    up_copy.start()

    peers = [device(z, xx, c) for xx in (left, right, far)]
    peers += [device(z_across, xx, c) for xx in (x, left, right, far)]
    near = list(peers)
    peers += [to_sibling, to_partner, to_partner_other]
    peers += [device(z, x, c, (g + d) % GROUPS) for d in (1, 2, 3)]
    barrier = pltpu.get_barrier_semaphore()
    for dev in peers:
        pl.semaphore_signal(barrier, inc=1, device_id=dev, device_id_type=MESH)
    pl.semaphore_wait(barrier, len(peers))

    def at(source, p):
        r, k = divmod(p, NK)
        return tok.at[source, pl.ds(START[r], PART[r]), pl.ds(KSTART[k], KCS[k])]

    def tok_send(source, p, n, cls, dev):
        send(at(source, p), at(source, p), tok_ss.at[n, p], tok_rs.at[cls, p], dev)

    s_left, s_right, s_far = bit * 4 + left, bit * 4 + right, bit * 4 + far
    other = (1 - bit) * 4
    a_mine, a_left, a_right, a_far = other + x, other + left, other + right, other + far

    def across_first(p):
        return p % 2 == 0

    def relay_right(p):
        return (p // 2) % 2 == 0

    sources = {
        LEFT: s_left, RIGHT: s_right, FAR: s_far, ACROSS: a_mine,
        ACROSS_LEFT: a_left, ACROSS_RIGHT: a_right, ACROSS_FAR: a_far,
    }

    def tok_arrived(cls, p):
        arrived(("tok", cls, p), at(sources[cls], p), tok_rs.at[cls, p])

    def own_piece(p):
        r, k = divmod(p, NK)
        return tok_hbm.at[pl.ds(START[r], PART[r]), pl.ds(KSTART[k], KCS[k])]

    def own_across(p):
        send(own_piece(p), at(mine, p), tok_ss.at[0, p], tok_rs.at[ACROSS, p], to_across)

    def own_sides(p):
        send(own_piece(p), at(mine, p), tok_ss.at[1, p], tok_rs.at[LEFT, p], to_right)
        send(own_piece(p), at(mine, p), tok_ss.at[2, p], tok_rs.at[RIGHT, p], to_left)

    def pass_across(p):
        tok_arrived(ACROSS, p)
        tok_send(a_mine, p, 3, ACROSS_LEFT, to_right)
        tok_send(a_mine, p, 4, ACROSS_RIGHT, to_left)

    def pass_left(p):
        tok_arrived(LEFT, p)
        if relay_right(p):
            tok_send(s_left, p, 5, FAR, to_right)
        if not across_first(p):
            tok_send(s_left, p, 3, ACROSS_LEFT, to_across)

    def pass_right(p):
        tok_arrived(RIGHT, p)
        if not relay_right(p):
            tok_send(s_right, p, 5, FAR, to_left)
        if not across_first(p):
            tok_send(s_right, p, 4, ACROSS_RIGHT, to_across)

    def pass_far(p):
        tok_arrived(FAR, p)
        tok_send(s_far, p, 6, ACROSS_FAR, to_across)

    def pass_across_left(p):
        tok_arrived(ACROSS_LEFT, p)
        tok_send(a_left, p, 6, ACROSS_FAR, to_right)

    def pass_across_right(p):
        tok_arrived(ACROSS_RIGHT, p)
        tok_send(a_right, p, 6, ACROSS_FAR, to_left)

    def tok_ready(r, k):
        once("own tokens", tok_copy)
        for cls in sources:
            tok_arrived(cls, r * NK + k)

    g_next, g_prev, g_far = (g + 1) % GROUPS, (g + 3) % GROUPS, (g + 2) % GROUPS
    to_next, to_prev = device(z, x, c, g_next), device(z, x, c, g_prev)
    w_quarters = (g, g_prev, g_far, g_next)

    def w_own(i):
        src, dst = w_own_at(i, g), w_at(2, i, g)
        send(src, dst, w_ss.at[0, i], w_rs.at[0, i], to_partner)

    def w_own_far(i):
        src, dst = w_own_at(i, g_far), w_at(2, i, g_far)
        send(src, dst, w_ss.at[3, i], w_rs.at[2, i], to_partner)

    def w_sibling(i):
        src, dst = w_own_at(i), w_at(1, i)
        send(src, dst, ws_ss.at[i], ws_rs.at[i], to_sibling)

    def w_arrived(cls, i):
        arrived(("w", cls, i), w_at(2, i, w_quarters[cls]), w_rs.at[cls, i])

    def w_forward(i, cls):
        src, dst = w_at(2, i, w_quarters[cls]), w_at(3, i, w_quarters[cls])
        send(src, dst, wf_ss.at[cls, i], wf_rs.at[cls, i], to_sibling)

    def w_send(i, q, n, cls, dev):
        ref = w_at(2, i, q)
        send(ref, ref, w_ss.at[n, i], w_rs.at[cls, i], dev)

    def w_pass(i):
        w_arrived(0, i)
        w_send(i, g, 1, 1, to_next)
        w_send(i, g, 2, 3, to_prev)
        w_forward(i, 0)

    def w_pass_prev(i):
        w_arrived(1, i)
        if i not in W_FAR_DIRECT and i % 2 == 0:
            w_send(i, g_prev, 3, 2, to_next)
        w_forward(i, 1)

    def w_pass_next(i):
        w_arrived(3, i)
        if i not in W_FAR_DIRECT and i % 2 == 1:
            w_send(i, g_next, 3, 2, to_prev)
        w_forward(i, 3)

    def w_pass_far(i):
        w_arrived(2, i)
        w_forward(i, 2)

    def w_ready(i):
        once(("own w", i), w_copies[i])
        arrived(("sibling w", i), w_at(1, i), ws_rs.at[i])
        for cls, q in enumerate(w_quarters):
            arrived(("other w", cls, i), w_at(3, i, q), wf_rs.at[cls, i])

    def picked_places():
        picked = []
        for dest in range(GROUPS):
            index = [jnp.int32(0)] * CAP
            count = jnp.int32(0)
            for j in range(REQUESTS):
                slot = slot_ref[rid_ref[dest, j]]
                is_mine = slot // OWNED == g
                local = slot % OWNED
                for p in range(min(CAP, j + 1)):
                    index[p] = jnp.where(is_mine & (count == p), local, index[p])
                count = count + is_mine.astype(jnp.int32)
            picked += index
        return picked

    def adapters_send(n, table, picks, gets):
        for p in range(GROUPS * CAP):
            picks[p] = table[picked[p]]
        for d in (1, 3, 2):
            rows = pl.ds(((g + d) % GROUPS) * CAP, CAP)
            dev = device(z, x, c, (g + d) % GROUPS)
            send(picks.at[rows], gets.at[pl.ds(g * CAP, CAP)], ad_ss.at[n, d], ad_rs.at[n, d], dev)
        rows = pl.ds(g * CAP, CAP)
        pltpu.make_async_copy(picks.at[rows], gets.at[rows], ad_ss.at[n, 0]).start()

    picked = []

    def down_pick():
        picked.extend(picked_places())
        down_copy.wait()
        adapters_send(0, dloc, dsend, drecv)
        tok_copy.start()
        for copy in w_copies:
            copy.start()

    def up_pick():
        up_copy.wait()
        adapters_send(1, uloc, usend, urecv)

    def request_places():
        places = []
        counts = [jnp.int32(0)] * GROUPS
        for j in range(REQUESTS):
            owner = slot_ref[rid_ref[g, j]] // OWNED
            place = jnp.int32(0)
            for o in range(GROUPS):
                hit = owner == o
                place = place + jnp.where(hit, o * CAP + counts[o], 0)
                counts[o] = counts[o] + hit.astype(jnp.int32)
            places.append(place)
        return places

    def adapters_arrived(n, ref, src):
        rows = pl.ds(g * CAP, CAP)
        pltpu.make_async_copy(src.at[rows], ref.at[rows], ad_ss.at[n, 0]).wait()
        for d in (1, 2, 3):
            rows = pl.ds(((g + 4 - d) % GROUPS) * CAP, CAP)
            arrived(("picked", n, d), ref.at[rows], ad_rs.at[n, d])

    def adapters_share(n, ref):
        send(ref.at[0], ref.at[2], cp_ss.at[n, 0], cp_rs.at[n, 2], to_partner)
        send(ref.at[0], ref.at[1], cp_ss.at[n, 1], cp_rs.at[n, 1], to_sibling)

    places = []

    def down_compact():
        places.extend(request_places())
        adapters_arrived(0, drecv, dsend)
        for j in range(REQUESTS):
            dtmp[2 * j : 2 * j + 2, :] = drecv[places[j]].astype(F32)
        dc[0] = dtmp[...].astype(BF16)
        adapters_share(0, dc)

    def up_compact():
        adapters_arrived(1, urecv, usend)
        for j in range(REQUESTS):
            uc[0, j] = urecv[places[j]]
        adapters_share(1, uc)

    def down_forward():
        adapters_forward(0, dc)

    def up_forward():
        adapters_forward(1, uc)

    def adapters_forward(n, ref):
        arrived(("adapters", n, 2), ref.at[2], cp_rs.at[n, 2])
        send(ref.at[2], ref.at[3], cp_ss.at[n, 2], cp_rs.at[n, 3], to_sibling)

    def adapters_ready(n, ref):
        arrived(("adapters", n, 1), ref.at[1], cp_rs.at[n, 1])
        arrived(("adapters", n, 3), ref.at[3], cp_rs.at[n, 3])

    begun = set()

    def add(key, ref, term):
        if key in begun:
            ref[...] += term
        else:
            begun.add(key)
            ref[...] = term

    def token_block(r, k):
        rows = tok[:, START[r] : START[r] + PART[r], KSTART[k] : KSTART[k] + KCS[k]]
        return rows.reshape(SOURCES * PART[r], KCS[k])

    def base(r, k, h):
        tok_ready(r, k)
        w_ready(h * NK + k)
        weight = wbuf[h, KSTART[k] : KSTART[k] + KCS[k], :]
        term = jnp.dot(token_block(r, k), weight, preferred_element_type=F32)
        add(("base", r, h), acc[r].at[h], term)

    def low_rank(r, k):
        tok_ready(r, k)
        adapters_ready(0, dc)
        rows = dc[:, :, KSTART[k] : KSTART[k] + KCS[k]].reshape(8 * REQUESTS, KCS[k])
        term = lax.dot_general(
            rows, token_block(r, k), (((1,), (1,)), ((), ())), preferred_element_type=F32
        )
        add(("low rank", r), part[r], term)

    ends = []
    total = jnp.int32(0)
    for j in range(REQUESTS):
        total = total + len_ref[g, j]
        ends.append(total)

    def request_of(row, r):
        source = jnp.zeros(row.shape, jnp.int32)
        for n in range(1, SOURCES):
            source = source + jnp.where(row >= n * PART[r], 1, 0)
        position = side * 1024 + source * 128 + c * SHARD + START[r] + row - source * PART[r]
        request = jnp.zeros(row.shape, jnp.int32)
        for j in range(REQUESTS):
            request = request + jnp.where(position >= ends[j], 1, 0)
        return request

    z_low = jnp.minimum(z, z_partner)
    quad = z_low * 4 + x

    first_late = []

    def requests_find(r):
        shape = (8 * REQUESTS, SOURCES * PART[r])
        by_lane[r][...] = request_of(lax.broadcasted_iota(jnp.int32, shape, 1), r)
        shape = (SOURCES * PART[r], 128)
        by_row[r][...] = request_of(lax.broadcasted_iota(jnp.int32, shape, 0), r)

    def codes_send(r):
        if r == PARTS - 1:
            first_late.append(len(sends))
        shape = (8 * REQUESTS, SOURCES * PART[r])
        row = lax.broadcasted_iota(jnp.int32, shape, 0)
        request = by_lane[r][...]
        masked = jnp.where(request == (row % 32) // 2, part[r][...], 0.0).astype(BF16)
        lane = lax.broadcasted_iota(jnp.int32, (16, 128), 1)
        member = lane // 32
        high = jnp.where(z == z_low, member // 2, 1 - member // 2)
        core = jnp.where(c == 0, member % 2, 1 - member % 2)
        place = high * 4 + core * 2 + lane % 2
        pick = jnp.where(place == lax.broadcasted_iota(jnp.int32, (16, 128), 0), 1.0, 0.0)
        codes = jnp.dot(pick.astype(BF16), masked, preferred_element_type=F32)
        shr[r][quad] = codes[:8]
        for n, dev in enumerate(near):
            cls = (RIGHT, LEFT, FAR, ACROSS, ACROSS_RIGHT, ACROSS_LEFT, ACROSS_FAR)[n]
            ref = shr[r].at[quad]
            send(ref, ref, sh_ss.at[r, n], sh_rs.at[r, cls], dev)

    def out_piece(zz, cc, r, h):
        rows, lanes = pl.ds(START[r], PART[r]), pl.ds(h * LANES, LANES)
        return out_hbm.at[zz // 2, :, cc, rows, lanes]

    def out_local(r, h):
        sem = loc_sem.at[3 + r * HALVES + h]
        return pltpu.make_async_copy(ost[r].at[h, 0], out_piece(z, c, r, h), sem)

    def codes_spread(r):
        if r == PARTS - 1:
            late = sends[first_late[0] :]
            del sends[first_late[0] :]
            sent()
            sends.extend(late)
        z_other_low = 1 - z_low
        quad_low, quad_other = z_low * 4, z_other_low * 4
        for cls, q in (
            (LEFT, quad_low + left), (RIGHT, quad_low + right), (FAR, quad_low + far),
            (ACROSS, quad_other + x), (ACROSS_LEFT, quad_other + left),
            (ACROSS_RIGHT, quad_other + right), (ACROSS_FAR, quad_other + far),
        ):
            arrived(("codes", r, cls), shr[r].at[q], sh_rs.at[r, cls])
        place = lax.broadcasted_iota(jnp.int32, (RANK, 128), 0)
        lane = lax.broadcasted_iota(jnp.int32, (RANK, 128), 1) % RANK
        low, xx, rest = place // 32, (place // 8) % 4, place % 8
        zz = jnp.where(rest // 4 == 0, low, 3 - low)
        rank = zz * 16 + xx * 4 + rest % 4
        order = jnp.where(rank == lane, 1.0, 0.0).astype(BF16)
        hrows = SOURCES * PART[r]
        codes = shr[r][...].reshape(RANK, hrows).astype(BF16)
        codes = lax.dot_general(codes, order, (((0,), (0,)), ((), ())), preferred_element_type=F32)
        request = by_row[r][...]
        half = lax.broadcasted_iota(jnp.int32, (hrows, 128), 1) // RANK
        request = request - half
        for b in range(REQUESTS // 2):
            block = jnp.where(request == 2 * b, codes, 0.0).astype(BF16)
            spread[r][:, b * 128 : (b + 1) * 128] = block

    def finish(r, h, pair):
        adapters_ready(1, uc)
        lanes = slice(h * LANES, (h + 1) * LANES)
        table = jnp.concatenate(
            [uc[m, :, :, lanes].reshape(REQUESTS * RANK, LANES) for m in (2 * pair, 2 * pair + 1)],
            axis=1,
        )
        update = jnp.dot(spread[r][...], table, preferred_element_type=F32)
        base_sum = acc[r][h, :, pair * 2 * LANES : (pair + 1) * 2 * LANES]
        result = (base_sum + 0.5 * update).astype(BF16)
        for n in (1, 0):
            m = 2 * pair + n
            piece = result[:, n * LANES : (n + 1) * LANES]
            ost[r][h, m] = piece.reshape(SOURCES, PART[r], LANES)
            if m == 0:
                out_local(r, h).start()
            else:
                dev = (None, to_sibling, to_partner, to_partner_other)[m]
                ss, rs = out_ss.at[r, h, m], out_rs.at[r, h, m]
                send(ost[r].at[h, m], out_piece(z, c, r, h), ss, rs, dev)

    def out_arrived(r, h):
        out_local(r, h).wait()
        for m, (zz, cc) in enumerate(((z, 1 - c), (z_partner, c), (z_partner, 1 - c)), 1):
            arrived(("out", r, h, m), out_piece(zz, cc, r, h), out_rs.at[r, h, m])

    order = [
        (own_sides, 0), (w_own, 1), (own_across, 0), (w_sibling, 1), (w_own_far, 6), (w_sibling, 6),
        (w_sibling, 3), (own_across, 1), (own_across, 2), (w_own, 3), (w_own, 4), (w_sibling, 5),
        (w_own, 0), (w_own, 2), (w_sibling, 4), (w_sibling, 2), (own_sides, 1), (own_sides, 2),
        (down_pick,), (w_pass, 1), (up_pick,), (requests_find, 0), (requests_find, 1), (own_across, 3), (own_sides, 3), (pass_across, 0),
        (w_sibling, 0), (w_own_far, 7), (w_sibling, 7), (pass_left, 0), (w_own, 7), (w_pass_far, 6),
        (w_own, 5), (w_own, 6), (own_across, 4), (pass_left, 1), (pass_right, 1), (down_compact,),
        (w_pass, 0), (pass_right, 2), (w_pass_prev, 1), (pass_across, 2), (w_pass_next, 1),
        (w_pass, 4), (pass_left, 3), (pass_right, 3), (pass_across, 4), (w_pass, 2),
        (w_pass_far, 7), (pass_across_left, 0), (w_pass, 7), (up_compact,), (own_across, 5),
        (w_pass, 3), (own_across, 6), (w_pass_next, 0), (w_pass_prev, 0), (own_across, 7),
        (w_pass_far, 1), (w_pass_prev, 4), (pass_far, 1), (pass_across_right, 2), (own_sides, 4),
        (w_pass_next, 4), (w_pass_prev, 2), (own_sides, 5), (own_sides, 6), (pass_far, 3),
        (w_pass_prev, 7), (w_pass_next, 2), (own_sides, 7), (pass_across_left, 4), (w_pass, 6),
        (w_pass_prev, 3), (w_pass_next, 7), (pass_across, 6), (down_forward,), (w_pass, 5),
        (w_pass_next, 3), (w_pass_far, 0), (low_rank, 0, 0), (pass_left, 4), (low_rank, 0, 2),
        (base, 0, 0, 0), (base, 0, 1, 0), (w_pass_far, 4), (w_pass_next, 6), (pass_left, 5),
        (pass_right, 5), (low_rank, 0, 1), (pass_right, 6), (base, 0, 0, 1), (w_pass_next, 5),
        (pass_left, 7), (pass_right, 7), (w_pass_far, 2), (low_rank, 0, 3), (codes_send, 0),
        (base, 0, 3, 1), (pass_across_right, 6), (base, 0, 2, 0), (w_pass_far, 3), (w_pass_prev, 6),
        (up_forward,), (pass_far, 7), (low_rank, 1, 0), (base, 0, 3, 0), (base, 1, 0, 0),
        (base, 1, 0, 1), (codes_spread, 0), (pass_far, 5), (base, 1, 2, 1), (finish, 0, 0, 1),
        (w_pass_prev, 5), (base, 1, 3, 0), (low_rank, 1, 2), (base, 1, 2, 0), (w_pass_far, 5),
        (low_rank, 1, 3), (base, 1, 3, 1), (base, 0, 2, 1), (low_rank, 1, 1), (codes_send, 1),
        (base, 0, 1, 1), (finish, 0, 1, 1), (base, 1, 1, 1), (base, 1, 1, 0), (finish, 0, 0, 0),
        (finish, 0, 1, 0), (codes_spread, 1), (finish, 1, 1, 1), (finish, 1, 0, 1),
        (finish, 1, 1, 0), (finish, 1, 0, 0),
    ]
    for action, *args in order:
        action(*args)
    for r in range(PARTS):
        for h in range(HALVES):
            out_arrived(r, h)
    sent()


def local(tokens, weight, down, up, lengths, request_adapter_id, adapter_storage_slot):
    dma = pltpu.SemaphoreType.DMA
    any_space = pl.BlockSpec(memory_space=pl.ANY)
    smem = pl.BlockSpec(memory_space=pltpu.SMEM)
    slots = GROUPS * CAP
    out = pl.pallas_call(
        kernel,
        out_shape=jax.ShapeDtypeStruct((2, SOURCES, 2, SHARD, COLS), BF16),
        in_specs=[any_space] * 4 + [smem] * 3,
        out_specs=any_space,
        scratch_shapes=[
            pltpu.VMEM((SOURCES, SHARD, WIDTH), BF16),
            pltpu.VMEM((HALVES, WIDTH, 4 * LANES), BF16),
            pltpu.VMEM((OWNED, 2, WIDTH), BF16),
            pltpu.VMEM((OWNED, RANK, COLS), BF16),
            pltpu.VMEM((slots, 2, WIDTH), BF16),
            pltpu.VMEM((slots, RANK, COLS), BF16),
            pltpu.VMEM((slots, 2, WIDTH), BF16),
            pltpu.VMEM((slots, RANK, COLS), BF16),
            pltpu.VMEM((2 * REQUESTS, WIDTH), F32),
            pltpu.VMEM((4, 2 * REQUESTS, WIDTH), BF16),
            pltpu.VMEM((4, REQUESTS, RANK, COLS), BF16),
            *(pltpu.VMEM((HALVES, SOURCES * n, 4 * LANES), F32) for n in PART),
            *(pltpu.VMEM((8 * REQUESTS, SOURCES * n), F32) for n in PART),
            *(pltpu.VMEM((SOURCES, 8, SOURCES * n), F32) for n in PART),
            *(pltpu.VMEM((SOURCES * n, REQUESTS * RANK), BF16) for n in PART),
            *(pltpu.VMEM((HALVES, 4, SOURCES, n, LANES), BF16) for n in PART),
            *(pltpu.VMEM((8 * REQUESTS, SOURCES * n), jnp.int32) for n in PART),
            *(pltpu.VMEM((SOURCES * n, 128), jnp.int32) for n in PART),
            dma((3 + PARTS * HALVES,)),
            dma((CHUNKS,)),
            dma((7, PIECES)),
            dma((7, PIECES)),
            dma((4, CHUNKS)),
            dma((4, CHUNKS)),
            dma((CHUNKS,)),
            dma((CHUNKS,)),
            dma((4, CHUNKS)),
            dma((4, CHUNKS)),
            dma((2, 4)),
            dma((2, 4)),
            dma((2, 3)),
            dma((2, 4)),
            dma((PARTS, 7)),
            dma((PARTS, 7)),
            dma((PARTS, HALVES, 4)),
            dma((PARTS, HALVES, 4)),
        ],
        compiler_params=pltpu.CompilerParams(
            collective_id=0, has_side_effects=True, vmem_limit_bytes=60 * 1024 * 1024
        ),
    )(tokens, weight, down, up, lengths, request_adapter_id, adapter_storage_slot)
    return out.reshape(2 * SOURCES * 2 * SHARD, COLS)


def solution(mesh):
    placed = (
        P(("group", "tp"), None),
        P(None, "tp"),
        P("group", "tp", None),
        P("group", None, "tp"),
        P(),
        P(),
        P(),
    )
    return jax.shard_map(
        local, mesh=mesh, in_specs=placed, out_specs=P("group", "tp"), check_vma=False
    )
```
